128 devices in a mesh: dp: 16 (over y_lo, x, core), tensor: 8 (over y_hi, z).
Axes of the slice: x: 4, y: 4 (y_hi: 2, y_lo: 2; y = y_hi * 2 + y_lo), z: 4, core: 2. Of those that a mesh axis runs over, the one named last changes fastest.
Arguments:
- picture_encoder_result: bfloat16 [5632, 1024], P('dp'), may hold values from -0.59765625 to 0.59765625
- sentence_encoder_result: bfloat16 [22528, 1024], P(('dp', 'tensor')), may hold values from -0.59765625 to 0.59765625
- picture_projector_matrix: bfloat16 [1024, 1024], P(None, 'tensor'), may hold values from -0.1875 to 0.1875
- sentence_projector_matrix: bfloat16 [1024, 1024], P(None, 'tensor'), may hold values from -0.1875 to 0.1875
- sentences_for_picture: int32 [5632], replicated, may hold values from 1 to 8, 22528 in all
- sharpness_factor: float32 [1], replicated, may hold values from 30 to 60
- score_offset_term: float32 [1], replicated, may hold values from -8 to -4
Outputs:
- grad_img: bfloat16 [5632, 1024], P('dp', 'tensor')
- grad_cap: bfloat16 [22528, 1024], P(('dp', 'tensor'))
The draws below stay inside these ranges and needn't reach their ends.
Inputs may be any that keep to these rules, and one draw needn't show every extreme that they name: The counts sum to 22528; the captions of image m are the consecutive rows start[m] to start[m] + sentences_for_picture[m] - 1 of sentence_encoder_result, where start[m] is the sum of the counts of images before m; some image has 8.
All inputs are finite; a program needn't handle non-finite values.
Results may differ from the reference program's by a relative error of at most 0.014.
Values may be sent and summed in bfloat16 or wider, within the bound.
A program may use at most 64 MiB of HBM per device.

```python
import math
import jax
import jax.numpy as jnp
import numpy as np
from jax import lax

D = 1024
E = 1024
IMG_DEV = 352
IMAGES = 5632
CAPS = 22528
N_DP = 16


def block_levels(own_key, shape, split, smallest, largest):
    factor_of = 1.0
    for dim, shards_of in split:
        heights = jax.random.uniform(jax.random.fold_in(jax.random.fold_in(own_key, 6), dim), (shards_of,), jnp.float32, smallest / len(split), largest / len(split))
        factor_of = factor_of * jnp.repeat(jnp.exp(heights), shape[dim] // shards_of).reshape((-1,) + (1,) * (len(shape) - 1 - dim))
    return factor_of


def length_profile(amount, total, reach, lean):
    weights = [(1 << 20) // math.isqrt(grade ** lean) + 1 for grade in range(2, amount + 1)]
    surplus, given = total - reach - (amount - 1), [1] * (amount - 1)
    while surplus > 0:
        movable = [i for i in range(amount - 1) if given[i] < reach]
        whole, budget = sum([weights[i] for i in movable]), surplus
        for i in movable:
            addition = min(reach - given[i], max(1, budget * weights[i] // whole), surplus)
            given[i] = given[i] + addition
            surplus = surplus - addition
    return np.array([reach] + given)


def uneven_parts(stream_key, count, total, reach, skew):
    if count == 2:
        one = jax.random.randint(stream_key, (), max(1, total - reach), min(reach, total - 1) + 1)
        return jnp.stack([one, total - one])
    sizes = jnp.asarray(length_profile(count, total, reach, skew), jnp.int32)
    couples = (count - 1) // 2
    donor, sink = sizes[1:1 + 2 * couples:2], sizes[2:2 + 2 * couples:2]
    slack = jnp.minimum(donor - 1, reach - sink)
    moved = jax.random.randint(jax.random.fold_in(stream_key, 1), (couples,), 0, 1 << 20) % (slack + 1)
    sizes = sizes.at[1:1 + 2 * couples:2].set(donor - moved).at[2:2 + 2 * couples:2].set(sink + moved)
    return sizes[jax.random.permutation(jax.random.fold_in(stream_key, 2), count)]


def bell_draw(stream_key, extent, width, bound, pieces=(), kind=jnp.bfloat16):
    gain = block_levels(stream_key, extent, pieces, -0.22, 0.18) if pieces else 1.0
    entries = jax.random.normal(stream_key, extent, jnp.float32) * width * gain
    return jnp.minimum(jnp.maximum(entries, -bound), bound).astype(kind)


def setup_inputs(seed: int = 0) -> dict:
    seeds = jax.random.split(jax.random.key(seed), 8)
    picture_encoder_result = bell_draw(seeds[0], (IMAGES, D), 0.1, 0.59765625, ((0, 16),))
    sentence_encoder_result = bell_draw(seeds[1], (CAPS, D), 0.1, 0.59765625, ((0, 128),))
    picture_projector_matrix = bell_draw(seeds[2], (D, E), D ** -0.5, 0.1875, ((1, 8),))
    sentence_projector_matrix = bell_draw(seeds[3], (D, E), D ** -0.5, 0.1875, ((1, 8),))
    sentences_for_picture = uneven_parts(seeds[4], IMAGES, CAPS, 8, 1).astype(jnp.int32)
    sharpness_factor = jnp.clip(jax.random.uniform(seeds[5], (1,), jnp.float32, 30.0, 60.0), 30.0, 60.0)
    score_offset_term = jnp.clip(jax.random.uniform(seeds[6], (1,), jnp.float32, -8.0, -4.0), -8.0, -4.0)
    return {"picture_encoder_result": picture_encoder_result, "sentence_encoder_result": sentence_encoder_result, "picture_projector_matrix": picture_projector_matrix, "sentence_projector_matrix": sentence_projector_matrix, "sentences_for_picture": sentences_for_picture, "sharpness_factor": sharpness_factor, "score_offset_term": score_offset_term}


epsilon = 1e-06

def embed(features, loss_multiplier):
    raw = jnp.dot(features, loss_multiplier, preferred_element_type=jnp.float32)
    scale = lax.rsqrt(lax.optimization_barrier(jnp.sum(raw * raw, axis=1, keepdims=True)) + epsilon)
    return (raw * scale, scale)

def scaling_factor(similarity_matrix, other_begin_list, sentence_tally_later, other_position, scaled_sharpness, displacement):
    raw_similarity = scaled_sharpness * similarity_matrix + displacement
    inside = (other_position >= other_begin_list) & (other_position < other_begin_list + sentence_tally_later)
    match_polarity = jnp.where(inside, 1.0, -1.0)
    loss_multiplier = jnp.where(inside, 1.0 / sentence_tally_later.astype(jnp.float32), 1.0)
    return (scaled_sharpness * (-match_polarity * loss_multiplier * jax.nn.sigmoid(-match_polarity * raw_similarity))).astype(jnp.bfloat16)

def unit_back(grad, unit, scale):
    return scale * (grad - unit * lax.optimization_barrier(jnp.sum(unit * grad, axis=1, keepdims=True)))

def reference(picture_encoder_result, sentence_encoder_result, picture_projector_matrix, sentence_projector_matrix, sentences_for_picture, sharpness_factor, score_offset_term):
    img_unit, img_scale = embed(picture_encoder_result, picture_projector_matrix)
    cap_unit, cap_scale = embed(sentence_encoder_result, sentence_projector_matrix)
    img_z = img_unit.astype(jnp.bfloat16)
    cap_z = cap_unit.astype(jnp.bfloat16)
    ends = jnp.cumsum(sentences_for_picture).astype(jnp.int32)
    starts = (ends - sentences_for_picture).astype(jnp.int32)
    sentence_number = jnp.arange(CAPS, dtype=jnp.int32)
    scaled_sharpness = sharpness_factor[0]
    displacement = score_offset_term[0]

    def scan_step(cap_grad, block):
        block_z, group_begin_list, group_sizes_list = block
        similarity_matrix = jnp.dot(block_z, cap_z.T, preferred_element_type=jnp.float32)
        pair_factor = scaling_factor(similarity_matrix, group_begin_list[:, None], group_sizes_list[:, None], sentence_number[None, :], scaled_sharpness, displacement)
        block_grad = jnp.dot(pair_factor, cap_z, preferred_element_type=jnp.float32)
        cap_grad = cap_grad + jnp.dot(pair_factor.T, block_z, preferred_element_type=jnp.float32)
        return (cap_grad, block_grad)
    cap_grad, img_grad = lax.scan(scan_step, jnp.zeros((CAPS, E), jnp.float32), (img_z.reshape(N_DP, IMG_DEV, E), starts.reshape(N_DP, IMG_DEV), sentences_for_picture.reshape(N_DP, IMG_DEV)))
    img_grad = img_grad.reshape(IMAGES, E)
    img_back = unit_back(img_grad, img_unit, img_scale)
    cap_back = unit_back(cap_grad, cap_unit, cap_scale)
    grad_img = jnp.dot(img_back, picture_projector_matrix.astype(jnp.float32).T, precision=lax.Precision.HIGHEST)
    grad_cap = jnp.dot(cap_back, sentence_projector_matrix.astype(jnp.float32).T, precision=lax.Precision.HIGHEST)
    return (grad_img.astype(jnp.bfloat16), grad_cap.astype(jnp.bfloat16))
```

```python
import jax
import jax.numpy as jnp
from jax import lax
from jax.experimental import pallas as pl
from jax.experimental.pallas import tpu as pltpu
from jax.sharding import PartitionSpec as P

EPS = 1e-06
LOG2E = 1.4426950408889634
MESH = pl.DeviceIdType.MESH
BF = jnp.bfloat16
F32 = jnp.float32

D = 1024
IMG = 352
PAD = 384
HALF = 176
CAP = 176
SL = 128
NT = (((1,), (1,)), ((), ()))
TN = (((0,), (0,)), ((), ()))


def mo(v, k):
    return pl.multiple_of(v, k)


def kernel(
    pic,
    sent,
    wp,
    ws,
    counts,
    sharp,
    bias,
    out_img,
    out_cap,
    wcap,
    wimg,
    plane,
    caps,
    coef,
    vecs,
    starts,
    part,
    own_cap,
    raw_cap,
    cap_in,
    cap_mid,
    img_send,
    img_recv,
    gp,
    gq,
    own_p,
    own_q,
    rpy,
    tpy,
    gp2,
    own_p2,
    rpz,
    tpz,
    rqz,
    tqz,
    gq2,
    own_q2,
    rqy,
    tqy,
    send_sem,
    recv_sem,
):
    dp = lax.axis_index("dp")
    tensor = lax.axis_index("tensor")
    c = dp % 2
    x = (dp // 2) % 4
    yl = dp // 8
    yh = tensor // 4
    z = tensor % 4
    y = yh * 2 + yl
    d = 1 - 2 * c

    def dev(x_, y_, z_, c_):
        return ((y_ % 2) * 8 + x_ * 2 + c_, (y_ // 2) * 4 + z_)

    def ring(v, s):
        return (v + 4 + s) % 4

    xf, xb = dev(ring(x, d), y, z, c), dev(ring(x, -d), y, z, c)
    yf, yb = dev(x, ring(y, d), z, c), dev(x, ring(y, -d), z, c)
    zf, zb = dev(x, y, ring(z, d), c), dev(x, y, ring(z, -d), c)
    core = dev(x, y, z, 1 - c)
    ym = dev(x, 3 - y, z, c)

    barrier = pltpu.get_barrier_semaphore()
    for other in (xf, xb, yf, yb, zf, zb, core):
        pl.semaphore_signal(barrier, inc=1, device_id=other, device_id_type=MESH)
    pl.semaphore_wait(barrier, 7)

    copies = []

    def make(src, dst, target):
        i = len(copies)
        copy = pltpu.make_async_remote_copy(
            src_ref=src,
            dst_ref=dst,
            send_sem=send_sem.at[i],
            recv_sem=recv_sem.at[i],
            device_id=target,
            device_id_type=MESH,
        )
        copies.append(copy)
        return copy

    def go(src, dst, target):
        copy = make(src, dst, target)
        copy.start()
        return copy

    hc = mo(c * 512, 512)

    def col(yh_, z_):
        return pl.ds(mo((yh_ * 4 + z_) * SL, SL), SL)

    def head_start(win, full):
        half = win.at[pl.ds(hc, 512)]
        here = full.at[pl.ds(hc, 512), col(yh, z)]
        st = {}
        st["f"] = go(half, here, zf)
        st["b"] = go(half, here, zb)
        st["m"] = go(half, here, ym)
        return st

    def piece(full, yh_, z_):
        return full.at[pl.ds(hc, 512), col(yh_, z_)]

    def same(full, yh_, z_, target):
        ref = piece(full, yh_, z_)
        return go(ref, ref, target)

    def head_mid(full, st):
        st["f"].wait_recv()
        st["ff"] = same(full, yh, ring(z, -d), zf)
        st["cores"] = [same(full, yh, ring(z, -d), core)]
        st["m"].wait_recv()
        st["mf"] = same(full, 1 - yh, z, zf)
        st["mb"] = same(full, 1 - yh, z, zb)
        st["cores"].append(same(full, 1 - yh, z, core))
        st["b"].wait_recv()
        st["cores"].append(same(full, yh, ring(z, d), core))

    def head_late(full, st):
        st["ff"].wait_recv()
        st["cores"].append(same(full, yh, ring(z, 2), core))
        st["mf"].wait_recv()
        st["mff"] = same(full, 1 - yh, ring(z, -d), zf)
        st["cores"].append(same(full, 1 - yh, ring(z, -d), core))
        st["mb"].wait_recv()
        st["cores"].append(same(full, 1 - yh, ring(z, d), core))

    def head_end(full, st):
        st["mff"].wait_recv()
        st["cores"].append(same(full, 1 - yh, ring(z, 2), core))
        for copy in st["cores"]:
            copy.wait_recv()

    cap_head = head_start(ws, wcap)
    wcap[:, col(yh, z)] = ws[...]

    k_own = yl * 2 + c
    zero = jnp.zeros((PAD - IMG, D), BF)
    for k in range(4):
        plane[k * PAD + IMG : (k + 1) * PAD, :] = zero
    plane[pl.ds(mo(k_own * PAD, PAD), IMG), col(yh, z)] = jnp.dot(
        pic[...], wp[...], preferred_element_type=F32
    ).astype(BF)

    def rows(y_, half):
        return pl.ds(mo(((y_ % 2) * 2 + c) * PAD + half * HALF, 16), HALF)

    def p_z(z_, target):
        ref = plane.at[rows(y, 0), col(yh, z_)]
        return go(ref, ref, target)

    def p_y(y_, target):
        ref = plane.at[rows(y_, 0), pl.ds(mo((y_ // 2) * 512, 512), 512)]
        return go(ref, ref, target)

    def q_y(y_, target):
        ref = plane.at[rows(y_, 1), col(y_ // 2, z)]
        return go(ref, ref, target)

    def q_z(z_, target):
        made = []
        for y_ in range(4):
            ref = plane.at[rows(y_, 1), col(y_ // 2, z_)]
            made.append(go(ref, ref, target))
        return made

    pzf, pzb = p_z(z, zf), p_z(z, zb)
    qyf, qyb = q_y(y, yf), q_y(y, yb)
    head_mid(wcap, cap_head)
    pzf.wait_recv()
    pzff = p_z(ring(z, -d), zf)
    qyf.wait_recv()
    qyff = q_y(ring(y, -d), yf)
    head_late(wcap, cap_head)
    pzb.wait_recv()
    pzff.wait_recv()
    pyf, pyb = p_y(y, yf), p_y(y, yb)
    qyb.wait_recv()
    qyff.wait_recv()
    qzf, qzb = q_z(z, zf), q_z(z, zb)
    head_end(wcap, cap_head)

    raw = jnp.dot(sent[...], wcap[...], preferred_element_type=F32)
    raw_cap[...] = raw
    cap_scale = lax.rsqrt(jnp.sum(raw * raw, axis=1, keepdims=True) + EPS)
    caps[0:CAP, :] = (raw * cap_scale).astype(BF)

    def cap_rows(slot):
        return caps.at[slot * CAP : (slot + 1) * CAP]

    cf = go(cap_rows(0), cap_rows(1), xf)
    cb = go(cap_rows(0), cap_rows(2), xb)
    img_head = head_start(wp, wimg)
    wimg[:, col(yh, z)] = wp[...]

    n = counts[...].astype(F32)
    nb = n.astype(BF)
    a = lax.broadcasted_iota(jnp.int32, (IMG, IMG), 0)
    b = lax.broadcasted_iota(jnp.int32, (IMG, IMG), 1)
    upto = jnp.dot(nb, (a < b).astype(F32).astype(BF), preferred_element_type=F32)
    a = lax.broadcasted_iota(jnp.int32, (16, 16), 0)
    b = lax.broadcasted_iota(jnp.int32, (16, 16), 1)
    before = jnp.dot((b < a).astype(F32).astype(BF), nb, preferred_element_type=F32)
    starts[0:16, 0:IMG] = upto + jnp.sum(before, axis=1, keepdims=True)
    starts[0:16, IMG:PAD] = jnp.full((16, PAD - IMG), -1.0, F32)
    starts[16:32, 0:IMG] = n
    starts[16:32, IMG:PAD] = jnp.full((16, PAD - IMG), 1.0, F32)

    pyf.wait_recv()
    pyff = p_y(ring(y, -d), yf)
    for copy in qzf:
        copy.wait_recv()
    qzff = q_z(ring(z, -d), zf)
    pyb.wait_recv()
    for copy in qzb:
        copy.wait_recv()
    pyff.wait_recv()
    for copy in qzff:
        copy.wait_recv()
    swaps = []
    for yl_ in range(2):
        ref = plane.at[pl.ds(mo((yl_ * 2 + c) * PAD, PAD), IMG)]
        swaps.append(go(ref, ref, core))
    head_mid(wimg, img_head)
    for copy in swaps:
        copy.wait_recv()
    head_late(wimg, img_head)

    t = sharp[0]
    shift = bias[0] * LOG2E
    ones = jnp.ones((8, D), BF)
    for yl_ in range(2):
        for c_ in range(2):
            k = yl_ * 2 + c_
            zk = plane[k * PAD : (k + 1) * PAD, :]
            square = lax.dot_general(ones, zk * zk, NT, preferred_element_type=F32)
            scale = t * lax.rsqrt(square[0:1, :] + EPS)
            row = (yl_ * 4 + x) * 2 + c_
            first = starts[pl.ds(row, 1), :]
            num = starts[pl.ds(16 + row, 1), :]
            lanes = slice(c_ * PAD, (c_ + 1) * PAD)
            vecs[yl_, 0:1, lanes] = scale * LOG2E
            vecs[yl_, 1:2, lanes] = scale
            vecs[yl_, 2:3, lanes] = -scale / num
            vecs[yl_, 3:4, lanes] = first
            vecs[yl_, 4:5, lanes] = jnp.where(first < 0.0, -1.0, first + num)

    cf.wait_recv()
    cff = go(cap_rows(1), cap_rows(3), xf)
    t3 = make(part.at[1], cap_in.at[2], xb)
    t1 = make(part.at[3], cap_in.at[0], xf)

    def one_slot(slot, carry):
        @pl.when(slot == 2)
        def _():
            cb.wait_recv()

        @pl.when(slot == 3)
        def _():
            cff.wait_recv()

        step = jnp.where(slot == 1, -d, jnp.where(slot == 2, d, 2 * (slot // 3)))
        there = ((yl * 4 + ring(x, step)) * 2 + c) * 8 + tensor
        r = pl.ds(mo(slot * CAP, CAP), CAP)
        number = (
            there * CAP + lax.broadcasted_iota(jnp.int32, (CAP, 2 * PAD), 0)
        ).astype(F32)
        total = jnp.zeros((CAP, D), F32)
        for yl_ in range(2):
            zy = plane[yl_ * 2 * PAD : (yl_ + 1) * 2 * PAD, :]
            s = lax.dot_general(caps[r, :], zy, NT, preferred_element_type=F32)
            l2 = s * vecs[yl_, 0:1, :] + shift
            inside = (number >= vecs[yl_, 3:4, :]) & (number < vecs[yl_, 4:5, :])
            e = jnp.exp2(jnp.where(inside, l2, -l2))
            w = jnp.where(inside, vecs[yl_, 2:3, :], vecs[yl_, 1:2, :])
            f = (w / (1.0 + e)).astype(BF)
            coef[yl_, r, :] = f
            total = total + jnp.dot(f, zy, preferred_element_type=F32)
        part[slot] = total.astype(BF)

        @pl.when(slot == 0)
        def _():
            own_cap[...] = total

        @pl.when(slot == 1)
        def _():
            t3.start()

        @pl.when(slot == 3)
        def _():
            t1.start()

        return carry

    lax.fori_loop(0, 4, one_slot, 0)
    head_end(wimg, img_head)

    def grad_rows(yl_, c_):
        f = coef[yl_, :, pl.ds(mo(c_ * PAD, PAD), PAD)]
        return lax.dot_general(f, caps[...], TN, preferred_element_type=F32)

    given = []
    for yl_ in range(2):
        img_send[yl_] = grad_rows(yl_, 1 - c)[0:IMG].astype(BF)
        given.append(go(img_send.at[yl_], img_recv.at[yl_], core))

    t1.wait_recv()
    cap_mid[...] = (part[2].astype(F32) + cap_in[0].astype(F32)).astype(BF)
    t2 = go(cap_mid, cap_in.at[1], xf)

    for yl_ in range(2):
        g = grad_rows(yl_, c)[0:IMG]
        given[yl_].wait_recv()
        g = g + img_recv[yl_].astype(F32)
        u = plane[pl.ds(mo((yl_ * 2 + c) * PAD, PAD), IMG), :].astype(F32)
        size = jnp.sum(u * u, axis=1, keepdims=True) + EPS
        along = jnp.sum(u * g, axis=1, keepdims=True)
        back = (g - u * (along / size)).astype(BF)
        grad = lax.dot_general(back, wimg[...], NT, preferred_element_type=F32)
        gp[yl_] = grad[0:HALF].astype(BF)
        for z_ in range(4):
            for yh_ in range(2):
                j = yh_ * 4 + z_
                at = (yh_ * 2 + yl_) * HALF
                gq[z_, at : at + HALF, :] = grad[
                    HALF:IMG, j * SL : (j + 1) * SL
                ].astype(BF)

    def gp_part(y_):
        return gp.at[y_ % 2, :, pl.ds(mo((y_ // 2) * 512, 512), 512)]

    py1 = go(gp_part(ring(y, 2)), rpy.at[0], yf)
    qz1 = go(gq.at[ring(z, 2)], rqz.at[0], zf)
    py3 = go(gp_part(ring(y, -d)), rpy.at[2], yb)
    qz3 = go(gq.at[ring(z, -d)], rqz.at[2], zb)

    def add(*refs):
        total = refs[0].astype(F32)
        for ref in refs[1:]:
            total = total + ref.astype(F32)
        return total

    py1.wait_recv()
    tpy[...] = add(gp_part(ring(y, d))[...], rpy[0]).astype(BF)
    py2 = go(tpy, rpy.at[1], yf)
    qz1.wait_recv()
    tqz[...] = add(gq[ring(z, d)], rqz[0]).astype(BF)
    qz2 = go(tqz, rqz.at[1], zf)

    t2.wait_recv()
    t3.wait_recv()
    g = own_cap[...] + cap_in[1].astype(F32) + cap_in[2].astype(F32)
    raw = raw_cap[...]
    cap_scale = lax.rsqrt(jnp.sum(raw * raw, axis=1, keepdims=True) + EPS)
    u = raw * cap_scale
    along = jnp.sum(u * g, axis=1, keepdims=True)
    back = (cap_scale * (g - u * along)).astype(BF)
    out_cap[...] = lax.dot_general(
        back, wcap[...], NT, preferred_element_type=F32
    ).astype(BF)

    py3.wait_recv()
    py2.wait_recv()
    own = add(gp_part(y)[...], rpy[1], rpy[2])
    for z_ in range(4):
        cut = own[:, z_ * SL : (z_ + 1) * SL]
        own_p2[z_] = cut
        gp2[z_] = cut.astype(BF)
    pz1 = go(gp2.at[ring(z, 2)], rpz.at[0], zf)
    pz3 = go(gp2.at[ring(z, -d)], rpz.at[2], zb)
    qz3.wait_recv()
    qz2.wait_recv()
    own = add(gq[z], rqz[1], rqz[2])
    for y_ in range(4):
        cut = own[y_ * HALF : (y_ + 1) * HALF]
        own_q2[y_] = cut
        gq2[y_] = cut.astype(BF)
    qy1 = go(gq2.at[ring(y, 2)], rqy.at[0], yf)
    qy3 = go(gq2.at[ring(y, -d)], rqy.at[2], yb)
    pz1.wait_recv()
    tpz[...] = (own_p2[ring(z, d)] + rpz[0].astype(F32)).astype(BF)
    pz2 = go(tpz, rpz.at[1], zf)
    qy1.wait_recv()
    tqy[...] = (own_q2[ring(y, d)] + rqy[0].astype(F32)).astype(BF)
    qy2 = go(tqy, rqy.at[1], yf)
    pz3.wait_recv()
    pz2.wait_recv()
    out_img[0:HALF, :] = (own_p2[z] + add(rpz[1], rpz[2])).astype(BF)
    qy3.wait_recv()
    qy2.wait_recv()
    out_img[HALF:IMG, :] = (own_q2[y] + add(rqy[1], rqy[2])).astype(BF)

    for copy in copies:
        copy.wait_send()


COPIES = 96


def body(pic, sent, wp, ws, counts, sharp, bias):
    vm = pl.BlockSpec(memory_space=pltpu.VMEM)
    sm = pl.BlockSpec(memory_space=pltpu.SMEM)
    scratch = [
        ((D, D), BF),
        ((D, D), BF),
        ((4 * PAD, D), BF),
        ((4 * CAP, D), BF),
        ((2, 4 * CAP, 2 * PAD), BF),
        ((2, 8, 2 * PAD), F32),
        ((32, PAD), F32),
        ((4, CAP, D), BF),
        ((CAP, D), F32),
        ((CAP, D), F32),
        ((3, CAP, D), BF),
        ((CAP, D), BF),
        ((2, IMG, D), BF),
        ((2, IMG, D), BF),
        ((2, HALF, D), BF),
        ((4, 4 * HALF, SL), BF),
        ((8, 128), F32),
        ((8, 128), F32),
        ((3, HALF, 512), BF),
        ((HALF, 512), BF),
        ((4, HALF, SL), BF),
        ((4, HALF, SL), F32),
        ((3, HALF, SL), BF),
        ((HALF, SL), BF),
        ((3, 4 * HALF, SL), BF),
        ((4 * HALF, SL), BF),
        ((4, HALF, SL), BF),
        ((4, HALF, SL), F32),
        ((3, HALF, SL), BF),
        ((HALF, SL), BF),
    ]
    return pl.pallas_call(
        kernel,
        out_shape=(
            jax.ShapeDtypeStruct((IMG, SL), BF),
            jax.ShapeDtypeStruct((CAP, D), BF),
        ),
        in_specs=[vm] * 5 + [sm] * 2,
        out_specs=(vm, vm),
        scratch_shapes=[pltpu.VMEM(shape, kind) for shape, kind in scratch]
        + [pltpu.SemaphoreType.DMA((COPIES,)), pltpu.SemaphoreType.DMA((COPIES,))],
        compiler_params=pltpu.CompilerParams(
            collective_id=0, has_side_effects=True, vmem_limit_bytes=56 * 1024 * 1024
        ),
    )(pic, sent, wp, ws, counts.reshape(16, IMG), sharp, bias)


def solution(mesh):
    in_specs = (
        P("dp", None),
        P(("dp", "tensor"), None),
        P(None, "tensor"),
        P(None, "tensor"),
        P(),
        P(),
        P(),
    )
    out_specs = (P("dp", "tensor"), P(("dp", "tensor"), None))
    return jax.shard_map(body, mesh=mesh, in_specs=in_specs, out_specs=out_specs, check_vma=False)
```

```python
import jax
import jax.numpy as jnp
from jax import lax
from jax.experimental import pallas as pl
from jax.experimental.pallas import tpu as pltpu
from jax.sharding import PartitionSpec as P

EPS = 1e-06
LOG2E = 1.4426950408889634
MESH = pl.DeviceIdType.MESH
BF = jnp.bfloat16
F32 = jnp.float32

D = 1024
IMG = 352
PAD = 384
HALF = 176
CUT = 256
CAP = 176
SL = 128
NT = (((1,), (1,)), ((), ()))
TN = (((0,), (0,)), ((), ()))


def mo(v, k):
    return pl.multiple_of(v, k)


def kernel(
    pic,
    sent,
    wp,
    ws,
    counts,
    sharp,
    bias,
    out_img,
    out_cap,
    pic_v,
    feat,
    wcap,
    wimg,
    plane,
    caps,
    coef,
    vecs,
    starts,
    part,
    own_cap,
    raw_cap,
    cap_in,
    cap_mid,
    img_send,
    img_own,
    img_recv,
    gp,
    gq,
    rpy,
    tpy,
    gp2,
    own_p2,
    rpz,
    rqz,
    tqz,
    gq2,
    own_q2,
    rqy,
    res_img,
    res_cap,
    send_sem,
    recv_sem,
    load_sem,
):
    dp = lax.axis_index("dp")
    tensor = lax.axis_index("tensor")
    c = dp % 2
    x = (dp // 2) % 4
    yl = dp // 8
    yh = tensor // 4
    z = tensor % 4
    y = yh * 2 + yl
    d = 1 - 2 * c

    def dev(x_, y_, z_, c_):
        return ((y_ % 2) * 8 + x_ * 2 + c_, (y_ // 2) * 4 + z_)

    def ring(v, s):
        return (v + 4 + s) % 4

    def col(yh_, z_):
        return pl.ds(mo((yh_ * 4 + z_) * SL, SL), SL)

    xf, xb = dev(ring(x, d), y, z, c), dev(ring(x, -d), y, z, c)
    yf, yb = dev(x, ring(y, d), z, c), dev(x, ring(y, -d), z, c)
    y2 = dev(x, ring(y, 2), z, c)
    zf, zb = dev(x, y, ring(z, d), c), dev(x, y, ring(z, -d), c)
    z2 = dev(x, y, ring(z, 2), c)
    core = dev(x, y, z, 1 - c)
    ym = dev(x, 3 - y, z, c)

    barrier = pltpu.get_barrier_semaphore()
    for other in (xf, xb, yf, yb, y2, zf, zb, z2, core):
        pl.semaphore_signal(barrier, inc=1, device_id=other, device_id_type=MESH)

    def load(i, src, dst):
        copy = pltpu.make_async_copy(src, dst, load_sem.at[i])
        copy.start()
        return copy

    load_pic = load(0, pic, pic_v)
    load_wp = load(1, wp, wimg.at[:, col(yh, z)])
    load_ws = load(2, ws, wcap.at[:, col(yh, z)])
    load_sent = load(3, sent, feat.at[3 * CAP : 4 * CAP])
    pl.semaphore_wait(barrier, 9)

    copies = []

    def make(src, dst, target):
        i = len(copies)
        copy = pltpu.make_async_remote_copy(
            src_ref=src,
            dst_ref=dst,
            send_sem=send_sem.at[i],
            recv_sem=recv_sem.at[i],
            device_id=target,
            device_id_type=MESH,
        )
        copies.append(copy)
        return copy

    def go(src, dst, target):
        copy = make(src, dst, target)
        copy.start()
        return copy

    hc = mo(c * 512, 512)

    def head_start(win, full):
        half = win.at[pl.ds(hc, 512)]
        here = full.at[pl.ds(hc, 512), col(yh, z)]
        st = {}
        st["m"] = go(half, here, ym)
        st["f"] = go(half, here, zf)
        st["b"] = go(half, here, zb)
        return st

    def same(full, yh_, z_, target):
        ref = full.at[pl.ds(hc, 512), col(yh_, z_)]
        return go(ref, ref, target)

    def head_mid(full, st):
        st["f"].wait_recv()
        st["ff"] = same(full, yh, ring(z, -d), zf)
        st["cores"] = [same(full, yh, ring(z, -d), core)]
        st["m"].wait_recv()
        st["mf"] = same(full, 1 - yh, z, zf)
        st["mb"] = same(full, 1 - yh, z, zb)
        st["cores"].append(same(full, 1 - yh, z, core))
        st["b"].wait_recv()
        st["cores"].append(same(full, yh, ring(z, d), core))

    def head_late(full, st):
        st["mf"].wait_recv()
        st["mff"] = same(full, 1 - yh, ring(z, -d), zf)
        st["cores"].append(same(full, 1 - yh, ring(z, -d), core))
        st["ff"].wait_recv()
        st["cores"].append(same(full, yh, ring(z, 2), core))
        st["mb"].wait_recv()
        st["cores"].append(same(full, 1 - yh, ring(z, d), core))

    def head_end(full, st):
        st["mff"].wait_recv()
        st["cores"].append(same(full, 1 - yh, ring(z, 2), core))
        for copy in st["cores"]:
            copy.wait_recv()

    cap_head = head_start(ws, wcap)

    def slot_rows(slot, lo, hi):
        return feat.at[slot * CAP + lo : slot * CAP + hi]

    xf1 = go(sent.at[0:96], slot_rows(1, 0, 96), xf)
    xb1 = go(sent, slot_rows(2, 0, CAP), xb)
    xf2 = go(sent.at[96:CAP], slot_rows(1, 96, CAP), xf)

    k_own = yl * 2 + c
    zero = jnp.zeros((PAD - IMG, D), BF)
    for k in range(4):
        plane[k * PAD + IMG : (k + 1) * PAD, :] = zero
    load_pic.wait()
    load_wp.wait()
    plane[pl.ds(mo(k_own * PAD, PAD), IMG), col(yh, z)] = jnp.dot(
        pic_v[...], wimg[:, col(yh, z)], preferred_element_type=F32
    ).astype(BF)

    def p_rows(y_):
        return pl.ds(mo(((y_ % 2) * 2 + c) * PAD, 16), CUT)

    def q_rows(y_):
        return pl.ds(mo(((y_ % 2) * 2 + c) * PAD + CUT, 16), IMG - CUT)

    def p_z(z_, target):
        ref = plane.at[p_rows(y), col(yh, z_)]
        return go(ref, ref, target)

    def p_y(y_, target):
        ref = plane.at[p_rows(y_), pl.ds(mo((y_ // 2) * 512, 512), 512)]
        return go(ref, ref, target)

    def q_y(y_, target):
        ref = plane.at[q_rows(y_), col(y_ // 2, z)]
        return go(ref, ref, target)

    def q_z(z_, target):
        made = []
        for y_ in range(4):
            ref = plane.at[q_rows(y_), col(y_ // 2, z_)]
            made.append(go(ref, ref, target))
        return made

    pzf, pzb = p_z(z, zf), p_z(z, zb)
    qyf, qyb = q_y(y, yf), q_y(y, yb)
    head_mid(wcap, cap_head)
    pzf.wait_recv()
    pzff = p_z(ring(z, -d), zf)
    qyf.wait_recv()
    qyff = q_y(ring(y, -d), yf)
    xf1.wait_recv()
    xff1 = go(slot_rows(1, 0, 96), slot_rows(0, 0, 96), xf)
    pzb.wait_recv()
    pzff.wait_recv()
    pyf, pyb = p_y(y, yf), p_y(y, yb)
    swaps = [p_y(y, core)]
    head_late(wcap, cap_head)
    qyb.wait_recv()
    qyff.wait_recv()
    qzf, qzb = q_z(z, zf), q_z(z, zb)
    xf2.wait_recv()
    xff2 = go(slot_rows(1, 96, CAP), slot_rows(0, 96, CAP), xf)

    n = counts[...].astype(F32)
    nb = n.astype(BF)
    a = lax.broadcasted_iota(jnp.int32, (128, 128), 0)
    b = lax.broadcasted_iota(jnp.int32, (128, 128), 1)
    upto = jnp.dot(nb, (a < b).astype(F32).astype(BF), preferred_element_type=F32)
    a = lax.broadcasted_iota(jnp.int32, (44, 44), 0)
    b = lax.broadcasted_iota(jnp.int32, (44, 44), 1)
    before = jnp.dot((b < a).astype(F32).astype(BF), nb, preferred_element_type=F32)
    starts[0, 0:44, :] = upto + jnp.sum(before, axis=1, keepdims=True)
    starts[1, 0:44, :] = n
    starts[0, 44:48, :] = jnp.full((4, 128), -1.0, F32)
    starts[1, 44:48, :] = jnp.full((4, 128), 1.0, F32)

    pyf.wait_recv()
    pyff = p_y(ring(y, -d), yf)
    swaps.append(p_y(ring(y, -d), core))
    for copy in qzf:
        copy.wait_recv()
    qzff = q_z(ring(z, -d), zf)
    head_end(wcap, cap_head)
    pyb.wait_recv()
    swaps.append(p_y(ring(y, d), core))
    for copy in qzb:
        copy.wait_recv()
    img_head = head_start(wp, wimg)

    load_ws.wait()
    load_sent.wait()

    def embed(rows):
        raw = jnp.dot(feat[rows, :], wcap[...], preferred_element_type=F32)
        cap_scale = lax.rsqrt(jnp.sum(raw * raw, axis=1, keepdims=True) + EPS)
        caps[rows, :] = (raw * cap_scale).astype(BF)
        return raw

    xb1.wait_recv()
    raw_cap[...] = embed(slice(2 * CAP, 4 * CAP))[CAP : 2 * CAP]
    pyff.wait_recv()
    swaps.append(p_y(ring(y, 2), core))
    for copy in qzff:
        copy.wait_recv()
    for yl_ in range(2):
        ref = plane.at[q_rows(yl_)]
        swaps.append(go(ref, ref, core))
    xff1.wait_recv()
    xff2.wait_recv()
    embed(slice(0, 2 * CAP))
    head_mid(wimg, img_head)
    for copy in swaps:
        copy.wait_recv()

    t = sharp[0]
    shift = bias[0] * LOG2E
    ones = jnp.ones((8, D), BF)
    even = x % 2 == 0

    def block_vec(which, yl_, c_):
        row = (yl_ * 4 + x) * 2 + c_
        q = (row * 11) // 4
        v = jnp.concatenate([starts[which, pl.ds(q + i, 1), :] for i in range(4)], axis=1)
        cuts = [((2 * p + 3 * c_) % 4) * 32 for p in range(2)]
        return jnp.where(even, v[:, cuts[0] : cuts[0] + PAD], v[:, cuts[1] : cuts[1] + PAD])

    for yl_ in range(2):
        for c_ in range(2):
            k = yl_ * 2 + c_
            zk = plane[k * PAD : (k + 1) * PAD, :]
            square = lax.dot_general(ones, zk * zk, NT, preferred_element_type=F32)
            scale = t * lax.rsqrt(square[0:1, :] + EPS)
            first = block_vec(0, yl_, c_)
            num = block_vec(1, yl_, c_)
            lanes = slice(c_ * PAD, (c_ + 1) * PAD)
            vecs[yl_, 0:1, lanes] = scale * LOG2E
            vecs[yl_, 1:2, lanes] = scale
            vecs[yl_, 2:3, lanes] = -scale / num
            vecs[yl_, 3:4, lanes] = first
            vecs[yl_, 4:5, lanes] = first + num

    t1 = make(part.at[0], cap_in.at[0], xf)
    t3 = make(part.at[1], cap_in.at[2], xb)

    def base(step):
        return (((yl * 4 + ring(x, step)) * 2 + c) * 8 + tensor) * CAP

    def two_slots(g, carry):
        low = jnp.where(g == 0, base(2), base(d))
        high = jnp.where(g == 0, base(-d), base(0))
        i = lax.broadcasted_iota(jnp.int32, (2 * CAP, 1), 0)
        number = (i + jnp.where(i < CAP, low, high - CAP)).astype(F32)
        r = pl.ds(mo(g * 2 * CAP, 2 * CAP), 2 * CAP)
        total = None
        for yl_ in range(2):
            zy = plane[yl_ * 2 * PAD : (yl_ + 1) * 2 * PAD, :]
            s = lax.dot_general(caps[r, :], zy, NT, preferred_element_type=F32)
            l2 = s * vecs[yl_, 0:1, :] + shift
            inside = (number >= vecs[yl_, 3:4, :]) & (number < vecs[yl_, 4:5, :])
            e = jnp.exp2(jnp.where(inside, l2, -l2))
            w = jnp.where(inside, vecs[yl_, 2:3, :], vecs[yl_, 1:2, :])
            f = (w / (1.0 + e)).astype(BF)
            coef[yl_, r, :] = f
            more = jnp.dot(f, zy, preferred_element_type=F32)
            total = more if total is None else total + more
        part[2 * g] = total[0:CAP].astype(BF)
        part[2 * g + 1] = total[CAP : 2 * CAP].astype(BF)

        @pl.when(g == 0)
        def _():
            t1.start()
            t3.start()

        @pl.when(g == 1)
        def _():
            own_cap[...] = total[CAP : 2 * CAP]

        return carry

    lax.fori_loop(0, 2, two_slots, 0)
    head_late(wimg, img_head)

    def grad_rows(yl_, c_):
        f = coef[yl_, :, pl.ds(mo(c_ * PAD, PAD), PAD)]
        return lax.dot_general(f, caps[...], TN, preferred_element_type=F32)

    given = []
    for i, yl_ in enumerate((yl, 1 - yl)):
        img_send[i] = grad_rows(yl_, 1 - c)[0:IMG].astype(BF)
        given.append(go(img_send.at[i], img_recv.at[i], core))
        if i == 0:
            img_own[0] = grad_rows(yl_, c)[0:IMG]
    img_own[1] = grad_rows(1 - yl, c)[0:IMG]
    t1.wait_recv()
    cap_mid[...] = (part[2].astype(F32) + cap_in[0].astype(F32)).astype(BF)
    t2 = go(cap_mid, cap_in.at[1], xf)
    head_end(wimg, img_head)

    def gp_part(y_):
        return gp.at[y_ % 2, :, pl.ds(mo((y_ // 2) * 512, 512), 512)]

    def image_back(i, yl_):
        given[i].wait_recv()
        g = img_own[i] + img_recv[i].astype(F32)
        u = plane[pl.ds(mo((yl_ * 2 + c) * PAD, PAD), IMG), :].astype(F32)
        size = jnp.sum(u * u, axis=1, keepdims=True) + EPS
        along = jnp.sum(u * g, axis=1, keepdims=True)
        back = (g - u * (along / size)).astype(BF)
        grad = lax.dot_general(back, wimg[...], NT, preferred_element_type=F32)
        gp[yl_] = grad[0:HALF].astype(BF)
        for z_ in range(4):
            for yh_ in range(2):
                j = yh_ * 4 + z_
                gq[z_, i, yh_ * HALF : (yh_ + 1) * HALF, :] = grad[
                    HALF:IMG, j * SL : (j + 1) * SL
                ].astype(BF)

    def add(*refs):
        total = refs[0].astype(F32)
        for ref in refs[1:]:
            total = total + ref.astype(F32)
        return total

    image_back(0, yl)
    py1 = go(gp_part(ring(y, 2)), rpy.at[0], yf)
    qz1 = [go(gq.at[ring(z, 2), 0], rqz.at[0, 0], zf)]
    qz3 = [go(gq.at[ring(z, -d), 0], rqz.at[2, 0], zb)]
    image_back(1, 1 - yl)
    py3 = go(gp_part(ring(y, -d)), rpy.at[2], yb)
    qz1.append(go(gq.at[ring(z, 2), 1], rqz.at[0, 1], zf))
    qz3.append(go(gq.at[ring(z, -d), 1], rqz.at[2, 1], zb))
    py1.wait_recv()
    tpy[...] = add(gp_part(ring(y, d))[...], rpy[0]).astype(BF)
    py2 = go(tpy, rpy.at[1], yf)
    qz2 = []
    for i in range(2):
        qz1[i].wait_recv()
        tqz[i] = add(gq[ring(z, d), i], rqz[0, i]).astype(BF)
        qz2.append(go(tqz.at[i], rqz.at[1, i], zf))

    t2.wait_recv()
    t3.wait_recv()
    g = own_cap[...] + cap_in[1].astype(F32) + cap_in[2].astype(F32)
    raw = raw_cap[...]
    cap_scale = lax.rsqrt(jnp.sum(raw * raw, axis=1, keepdims=True) + EPS)
    u = raw * cap_scale
    along = jnp.sum(u * g, axis=1, keepdims=True)
    back = (cap_scale * (g - u * along)).astype(BF)
    res_cap[...] = lax.dot_general(
        back, wcap[...], NT, preferred_element_type=F32
    ).astype(BF)
    store_cap = load(4, res_cap, out_cap)

    py3.wait_recv()
    py2.wait_recv()
    own = add(gp_part(y)[...], rpy[1], rpy[2])
    for z_ in range(4):
        cut = own[:, z_ * SL : (z_ + 1) * SL]
        own_p2[z_] = cut
        gp2[z_] = cut.astype(BF)
    pz = [
        go(gp2.at[ring(z, 2)], rpz.at[0], z2),
        go(gp2.at[ring(z, d)], rpz.at[1], zf),
        go(gp2.at[ring(z, -d)], rpz.at[2], zb),
    ]
    for i in range(2):
        qz3[i].wait_recv()
        qz2[i].wait_recv()
        own = add(gq[z, i], rqz[1, i], rqz[2, i])
        for yh_ in range(2):
            cut = own[yh_ * HALF : (yh_ + 1) * HALF]
            own_q2[i, yh_] = cut
            gq2[i, yh_] = cut.astype(BF)

    def q2(ref, y_):
        return ref.at[(y_ + y) % 2, y_ // 2]

    qy = [
        go(q2(gq2, ring(y, 2)), rqy.at[0], y2),
        go(q2(gq2, ring(y, d)), rqy.at[1], yf),
        go(q2(gq2, ring(y, -d)), rqy.at[2], yb),
    ]
    for copy in pz:
        copy.wait_recv()
    res_img[0:HALF, :] = (own_p2[z] + add(rpz[0], rpz[1], rpz[2])).astype(BF)
    for copy in qy:
        copy.wait_recv()
    res_img[HALF:IMG, :] = (own_q2[0, yh] + add(rqy[0], rqy[1], rqy[2])).astype(BF)
    store_img = load(5, res_img, out_img)
    for copy in copies:
        copy.wait_send()
    store_cap.wait()
    store_img.wait()


def finish(img, cap, out_img, out_cap):
    out_img[...] = img[...]
    out_cap[...] = cap[...]


COPIES = 96


def body(pic, sent, wp, ws, counts, sharp, bias):
    vm = pl.BlockSpec(memory_space=pltpu.VMEM)
    sm = pl.BlockSpec(memory_space=pltpu.SMEM)
    hbm = pl.BlockSpec(memory_space=pl.ANY)
    scratch = [
        ((IMG, D), BF),
        ((4 * CAP, D), BF),
        ((D, D), BF),
        ((D, D), BF),
        ((4 * PAD, D), BF),
        ((4 * CAP, D), BF),
        ((2, 4 * CAP, 2 * PAD), BF),
        ((2, 8, 2 * PAD), F32),
        ((2, 48, 128), F32),
        ((4, CAP, D), BF),
        ((CAP, D), F32),
        ((CAP, D), F32),
        ((3, CAP, D), BF),
        ((CAP, D), BF),
        ((2, IMG, D), BF),
        ((2, IMG, D), F32),
        ((2, IMG, D), BF),
        ((2, HALF, D), BF),
        ((4, 2, 2 * HALF, SL), BF),
        ((3, HALF, 512), BF),
        ((HALF, 512), BF),
        ((4, HALF, SL), BF),
        ((4, HALF, SL), F32),
        ((3, HALF, SL), BF),
        ((3, 2, 2 * HALF, SL), BF),
        ((2, 2 * HALF, SL), BF),
        ((2, 2, HALF, SL), BF),
        ((2, 2, HALF, SL), F32),
        ((3, HALF, SL), BF),
        ((IMG, SL), BF),
        ((CAP, D), BF),
    ]
    outs = (
        jax.ShapeDtypeStruct((IMG, SL), BF),
        jax.ShapeDtypeStruct((CAP, D), BF),
    )
    img, cap = pl.pallas_call(
        kernel,
        out_shape=outs,
        in_specs=[hbm] * 4 + [vm] + [sm] * 2,
        out_specs=(hbm, hbm),
        scratch_shapes=[pltpu.VMEM(shape, kind) for shape, kind in scratch]
        + [
            pltpu.SemaphoreType.DMA((COPIES,)),
            pltpu.SemaphoreType.DMA((COPIES,)),
            pltpu.SemaphoreType.DMA((6,)),
        ],
        compiler_params=pltpu.CompilerParams(
            collective_id=0, has_side_effects=True, vmem_limit_bytes=58 * 1024 * 1024
        ),
    )(pic, sent, wp, ws, counts.reshape(44, 128), sharp, bias)
    return pl.pallas_call(
        finish, out_shape=outs, in_specs=[vm, vm], out_specs=(vm, vm)
    )(img, cap)


def solution(mesh):
    in_specs = (
        P("dp", None),
        P(("dp", "tensor"), None),
        P(None, "tensor"),
        P(None, "tensor"),
        P(),
        P(),
        P(),
    )
    out_specs = (P("dp", "tensor"), P(("dp", "tensor"), None))
    return jax.shard_map(body, mesh=mesh, in_specs=in_specs, out_specs=out_specs, check_vma=False)
```

```python
import jax
import jax.numpy as jnp
from jax import lax
from jax.experimental import pallas as pl
from jax.experimental.pallas import tpu as pltpu
from jax.sharding import PartitionSpec as P

EPS = 1e-06
LOG2E = 1.4426950408889634
MESH = pl.DeviceIdType.MESH
BF = jnp.bfloat16
F32 = jnp.float32

D = 1024
IMG = 352
PAD = 384
HALF = 176
CUT = 256
CAP = 176
SL = 128
NT = (((1,), (1,)), ((), ()))
TN = (((0,), (0,)), ((), ()))


def mo(v, k):
    return pl.multiple_of(v, k)


def kernel(
    pic,
    sent,
    wp,
    ws,
    counts,
    sharp,
    bias,
    out_img,
    out_cap,
    pic_v,
    feat,
    wcap,
    wimg,
    plane,
    caps,
    coef,
    vecs,
    starts,
    part,
    own_cap,
    raw_cap,
    cap_in,
    cap_mid,
    img_send,
    img_own,
    img_recv,
    gp,
    gq,
    rpy,
    tpy,
    gp2,
    own_p2,
    rpz,
    rqz,
    tqz,
    gq2,
    own_q2,
    rqy,
    res_img,
    res_cap,
    send_sem,
    recv_sem,
    load_sem,
):
    dp = lax.axis_index("dp")
    tensor = lax.axis_index("tensor")
    c = dp % 2
    x = (dp // 2) % 4
    yl = dp // 8
    yh = tensor // 4
    z = tensor % 4
    y = yh * 2 + yl
    d = 1 - 2 * c

    def dev(x_, y_, z_, c_):
        return ((y_ % 2) * 8 + x_ * 2 + c_, (y_ // 2) * 4 + z_)

    def ring(v, s):
        return (v + 4 + s) % 4

    def col(yh_, z_):
        return pl.ds(mo((yh_ * 4 + z_) * SL, SL), SL)

    xf, xb = dev(ring(x, d), y, z, c), dev(ring(x, -d), y, z, c)
    yf, yb = dev(x, ring(y, d), z, c), dev(x, ring(y, -d), z, c)
    y2 = dev(x, ring(y, 2), z, c)
    zf, zb = dev(x, y, ring(z, d), c), dev(x, y, ring(z, -d), c)
    z2 = dev(x, y, ring(z, 2), c)
    core = dev(x, y, z, 1 - c)
    ym = dev(x, 3 - y, z, c)

    barrier = pltpu.get_barrier_semaphore()
    for other in (xf, xb, yf, yb, y2, zf, zb, z2, core):
        pl.semaphore_signal(barrier, inc=1, device_id=other, device_id_type=MESH)

    def load(i, src, dst):
        copy = pltpu.make_async_copy(src, dst, load_sem.at[i])
        copy.start()
        return copy

    load_pic = load(0, pic, pic_v)
    load_wp = load(1, wp, wimg.at[:, col(yh, z)])
    load_ws = load(2, ws, wcap.at[:, col(yh, z)])
    load_sent = load(3, sent, feat.at[3 * CAP : 4 * CAP])

    copies = []

    def make(src, dst, target):
        i = len(copies)
        copy = pltpu.make_async_remote_copy(
            src_ref=src,
            dst_ref=dst,
            send_sem=send_sem.at[i],
            recv_sem=recv_sem.at[i],
            device_id=target,
            device_id_type=MESH,
        )
        copies.append(copy)
        return copy

    def go(src, dst, target):
        copy = make(src, dst, target)
        copy.start()
        return copy

    k_own = yl * 2 + c
    zero = jnp.zeros((PAD - IMG, D), BF)
    for k in range(4):
        plane[k * PAD + IMG : (k + 1) * PAD, :] = zero
    load_wp.wait()
    load_pic.wait()
    plane[pl.ds(mo(k_own * PAD, PAD), IMG), col(yh, z)] = jnp.dot(
        pic_v[...], wimg[:, col(yh, z)], preferred_element_type=F32
    ).astype(BF)
    pl.semaphore_wait(barrier, 9)

    def p_rows(y_, lo=0, num=CUT):
        return pl.ds(mo(((y_ % 2) * 2 + c) * PAD + lo, 16), num)

    def q_rows(y_):
        return pl.ds(mo(((y_ % 2) * 2 + c) * PAD + CUT, 16), IMG - CUT)

    def p_z(z_, target):
        ref = plane.at[p_rows(y), col(yh, z_)]
        return go(ref, ref, target)

    def p_y(y_, target, lo=0, num=CUT):
        ref = plane.at[p_rows(y_, lo, num), pl.ds(mo((y_ // 2) * 512, 512), 512)]
        return go(ref, ref, target)

    def q_y(y_, target):
        ref = plane.at[q_rows(y_), col(y_ // 2, z)]
        return go(ref, ref, target)

    def q_z(z_, target):
        made = []
        for y_ in range(4):
            ref = plane.at[q_rows(y_), col(y_ // 2, z_)]
            made.append(go(ref, ref, target))
        return made

    hc = mo(c * 512, 512)

    def head_start(win, full, straight):
        half = win.at[pl.ds(hc, 512)]
        here = full.at[pl.ds(hc, 512), col(yh, z)]
        st = {"m": go(half, here, ym), "f": go(half, here, zf), "b": go(half, here, zb)}
        if straight:
            st["2"] = go(half, here, z2)
        return st

    def same(full, yh_, z_, target, start=True):
        ref = full.at[pl.ds(hc, 512), col(yh_, z_)]
        return (go if start else make)(ref, ref, target)

    def slot_rows(slot, lo, hi):
        return feat.at[slot * CAP + lo : slot * CAP + hi]

    pz = [p_z(z, target) for target in (zf, zb, z2)]
    qy = [q_y(y, target) for target in (yf, yb, y2)]
    head = head_start(ws, wcap, False)
    xf1 = go(sent.at[0:96], slot_rows(1, 0, 96), xf)
    xb1 = go(sent, slot_rows(2, 0, CAP), xb)
    xf2 = go(sent.at[96:CAP], slot_rows(1, 96, CAP), xf)

    for copy in qy:
        copy.wait_recv()
    qzf, qzb = q_z(z, zf), q_z(z, zb)
    for copy in pz:
        copy.wait_recv()
    pyf0 = p_y(y, yf, 0, CUT // 2)
    pyb = p_y(y, yb)
    pyf1 = p_y(y, yf, CUT // 2, CUT // 2)
    swaps = [p_y(y, core)]
    head["m"].wait_recv()
    head_mf = same(wcap, 1 - yh, z, zf)
    head_mb = same(wcap, 1 - yh, z, zb)
    cores = [same(wcap, 1 - yh, z, core)]
    head["f"].wait_recv()
    head_ff = same(wcap, yh, ring(z, -d), zf)
    cores.append(same(wcap, yh, ring(z, -d), core))
    xf1.wait_recv()
    xff1 = go(slot_rows(1, 0, 96), slot_rows(0, 0, 96), xf)
    pyf0.wait_recv()
    pyff0 = p_y(ring(y, -d), yf, 0, CUT // 2)
    head["b"].wait_recv()
    cores.append(same(wcap, yh, ring(z, d), core))
    for copy in qzf:
        copy.wait_recv()
    qzff = q_z(ring(z, -d), zf)
    head_mf.wait_recv()
    head_mff = same(wcap, 1 - yh, ring(z, -d), zf)
    cores.append(same(wcap, 1 - yh, ring(z, -d), core))
    xf2.wait_recv()
    xff2 = go(slot_rows(1, 96, CAP), slot_rows(0, 96, CAP), xf)
    pyf1.wait_recv()
    pyff1 = p_y(ring(y, -d), yf, CUT // 2, CUT // 2)
    swaps.append(p_y(ring(y, -d), core))

    n = counts[...].astype(F32)
    nb = n.astype(BF)
    a = lax.broadcasted_iota(jnp.int32, (128, 128), 0)
    b = lax.broadcasted_iota(jnp.int32, (128, 128), 1)
    upto = jnp.dot(nb, (a < b).astype(F32).astype(BF), preferred_element_type=F32)
    a = lax.broadcasted_iota(jnp.int32, (44, 44), 0)
    b = lax.broadcasted_iota(jnp.int32, (44, 44), 1)
    before = jnp.dot((b < a).astype(F32).astype(BF), nb, preferred_element_type=F32)
    starts[0, 0:44, :] = upto + jnp.sum(before, axis=1, keepdims=True)
    starts[1, 0:44, :] = n
    starts[0, 44:48, :] = jnp.full((4, 128), -1.0, F32)
    starts[1, 44:48, :] = jnp.full((4, 128), 1.0, F32)

    head_ff.wait_recv()
    cores.append(same(wcap, yh, ring(z, 2), core))
    head_mb.wait_recv()
    cores.append(same(wcap, 1 - yh, ring(z, d), core))
    pyb.wait_recv()
    swaps.append(p_y(ring(y, d), core))
    head_mff.wait_recv()
    cores.append(same(wcap, 1 - yh, ring(z, 2), core))
    ihead = head_start(wp, wimg, True)
    for copy in cores:
        copy.wait_recv()

    load_ws.wait()
    load_sent.wait()

    def embed(rows):
        raw = jnp.dot(feat[rows, :], wcap[...], preferred_element_type=F32)
        cap_scale = lax.rsqrt(jnp.sum(raw * raw, axis=1, keepdims=True) + EPS)
        caps[rows, :] = (raw * cap_scale).astype(BF)
        return raw

    xb1.wait_recv()
    raw_cap[...] = embed(slice(2 * CAP, 4 * CAP))[CAP : 2 * CAP]
    pyff0.wait_recv()
    pyff1.wait_recv()
    swaps.append(p_y(ring(y, 2), core))
    for copy in qzb + qzff:
        copy.wait_recv()
    for yl_ in range(2):
        ref = plane.at[q_rows(yl_)]
        swaps.append(go(ref, ref, core))
    xff1.wait_recv()
    xff2.wait_recv()
    embed(slice(0, 2 * CAP))
    ihead["m"].wait_recv()
    ihead_m = [same(wimg, 1 - yh, z, target) for target in (zf, zb, z2)]
    icores = [same(wimg, 1 - yh, z, core)]
    for name, step in (("f", -d), ("b", d), ("2", 2)):
        ihead[name].wait_recv()
        icores.append(same(wimg, yh, ring(z, step), core))
    icores_late = [same(wimg, 1 - yh, ring(z, step), core, False) for step in (-d, d, 2)]
    for copy in swaps:
        copy.wait_recv()

    t = sharp[0]
    shift = bias[0] * LOG2E
    ones = jnp.ones((8, D), BF)
    even = x % 2 == 0

    def block_vec(which, yl_, c_):
        row = (yl_ * 4 + x) * 2 + c_
        q = (row * 11) // 4
        v = jnp.concatenate([starts[which, pl.ds(q + i, 1), :] for i in range(4)], axis=1)
        cuts = [((2 * p + 3 * c_) % 4) * 32 for p in range(2)]
        return jnp.where(even, v[:, cuts[0] : cuts[0] + PAD], v[:, cuts[1] : cuts[1] + PAD])

    for yl_ in range(2):
        for c_ in range(2):
            k = yl_ * 2 + c_
            zk = plane[k * PAD : (k + 1) * PAD, :]
            square = lax.dot_general(ones, zk * zk, NT, preferred_element_type=F32)
            scale = t * lax.rsqrt(square[0:1, :] + EPS)
            first = block_vec(0, yl_, c_)
            num = block_vec(1, yl_, c_)
            lanes = slice(c_ * PAD, (c_ + 1) * PAD)
            vecs[yl_, 0:1, lanes] = scale * LOG2E
            vecs[yl_, 1:2, lanes] = scale
            vecs[yl_, 2:3, lanes] = -scale / num
            vecs[yl_, 3:4, lanes] = first
            vecs[yl_, 4:5, lanes] = first + num

    t1 = make(part.at[0], cap_in.at[0], xf)
    t3 = make(part.at[1], cap_in.at[2], xb)

    def base(step):
        return (((yl * 4 + ring(x, step)) * 2 + c) * 8 + tensor) * CAP

    def two_slots(g, carry):
        low = jnp.where(g == 0, base(2), base(d))
        high = jnp.where(g == 0, base(-d), base(0))
        i = lax.broadcasted_iota(jnp.int32, (2 * CAP, 1), 0)
        number = (i + jnp.where(i < CAP, low, high - CAP)).astype(F32)
        r = pl.ds(mo(g * 2 * CAP, 2 * CAP), 2 * CAP)
        total = None
        for yl_ in range(2):
            zy = plane[yl_ * 2 * PAD : (yl_ + 1) * 2 * PAD, :]
            s = lax.dot_general(caps[r, :], zy, NT, preferred_element_type=F32)
            l2 = s * vecs[yl_, 0:1, :] + shift
            inside = (number >= vecs[yl_, 3:4, :]) & (number < vecs[yl_, 4:5, :])
            e = jnp.exp2(jnp.where(inside, l2, -l2))
            w = jnp.where(inside, vecs[yl_, 2:3, :], vecs[yl_, 1:2, :])
            f = (w / (1.0 + e)).astype(BF)
            coef[yl_, r, :] = f
            more = jnp.dot(f, zy, preferred_element_type=F32)
            total = more if total is None else total + more
        part[2 * g] = total[0:CAP].astype(BF)
        part[2 * g + 1] = total[CAP : 2 * CAP].astype(BF)

        @pl.when(g == 0)
        def _():
            t1.start()

        @pl.when(g == 1)
        def _():
            own_cap[...] = total[CAP : 2 * CAP]
            t3.start()
            for arrived, copy in zip(ihead_m, icores_late):
                arrived.wait_recv()
                copy.start()

        return carry

    lax.fori_loop(0, 2, two_slots, 0)

    def grad_rows(yl_, c_):
        f = coef[yl_, :, pl.ds(mo(c_ * PAD, PAD), PAD)]
        return lax.dot_general(f, caps[...], TN, preferred_element_type=F32)

    given = []
    for i, yl_ in enumerate((yl, 1 - yl)):
        img_send[i] = grad_rows(yl_, 1 - c)[0:IMG].astype(BF)
        given.append(go(img_send.at[i], img_recv.at[i], core))
        if i == 0:
            img_own[0] = grad_rows(yl_, c)[0:IMG]
    for copy in icores + icores_late:
        copy.wait_recv()

    def gp_part(y_):
        return gp.at[y_ % 2, :, pl.ds(mo((y_ // 2) * 512, 512), 512)]

    def image_back(i, yl_):
        given[i].wait_recv()
        g = img_own[i] + img_recv[i].astype(F32)
        u = plane[pl.ds(mo((yl_ * 2 + c) * PAD, PAD), IMG), :].astype(F32)
        size = jnp.sum(u * u, axis=1, keepdims=True) + EPS
        along = jnp.sum(u * g, axis=1, keepdims=True)
        back = (g - u * (along / size)).astype(BF)
        grad = lax.dot_general(back, wimg[...], NT, preferred_element_type=F32)
        gp[yl_] = grad[0:HALF].astype(BF)
        for z_ in range(4):
            for yh_ in range(2):
                j = yh_ * 4 + z_
                gq[z_, i, yh_ * HALF : (yh_ + 1) * HALF, :] = grad[
                    HALF:IMG, j * SL : (j + 1) * SL
                ].astype(BF)

    def add(*refs):
        total = refs[0].astype(F32)
        for ref in refs[1:]:
            total = total + ref.astype(F32)
        return total

    image_back(0, yl)
    py1 = go(gp_part(ring(y, 2)), rpy.at[0], yf)
    qz1 = [go(gq.at[ring(z, 2), 0], rqz.at[0, 0], zf)]
    qz3 = [go(gq.at[ring(z, -d), 0], rqz.at[2, 0], zb)]
    img_own[1] = grad_rows(1 - yl, c)[0:IMG]
    t1.wait_recv()
    cap_mid[...] = (part[2].astype(F32) + cap_in[0].astype(F32)).astype(BF)
    t2 = go(cap_mid, cap_in.at[1], xf)
    image_back(1, 1 - yl)
    py3 = go(gp_part(ring(y, -d)), rpy.at[2], yb)
    qz1.append(go(gq.at[ring(z, 2), 1], rqz.at[0, 1], zf))
    qz3.append(go(gq.at[ring(z, -d), 1], rqz.at[2, 1], zb))
    py1.wait_recv()
    tpy[...] = add(gp_part(ring(y, d))[...], rpy[0]).astype(BF)
    py2 = go(tpy, rpy.at[1], yf)
    qz2 = []
    for i in range(2):
        qz1[i].wait_recv()
        tqz[i] = add(gq[ring(z, d), i], rqz[0, i]).astype(BF)
        qz2.append(go(tqz.at[i], rqz.at[1, i], zf))

    t2.wait_recv()
    t3.wait_recv()
    g = own_cap[...] + cap_in[1].astype(F32) + cap_in[2].astype(F32)
    raw = raw_cap[...]
    cap_scale = lax.rsqrt(jnp.sum(raw * raw, axis=1, keepdims=True) + EPS)
    u = raw * cap_scale
    along = jnp.sum(u * g, axis=1, keepdims=True)
    back = (cap_scale * (g - u * along)).astype(BF)
    res_cap[...] = lax.dot_general(
        back, wcap[...], NT, preferred_element_type=F32
    ).astype(BF)
    store_cap = load(4, res_cap, out_cap)

    py3.wait_recv()
    py2.wait_recv()
    own = add(gp_part(y)[...], rpy[1], rpy[2])
    for z_ in range(4):
        cut = own[:, z_ * SL : (z_ + 1) * SL]
        own_p2[z_] = cut
        gp2[z_] = cut.astype(BF)
    pz = [
        go(gp2.at[ring(z, 2)], rpz.at[0], z2),
        go(gp2.at[ring(z, d)], rpz.at[1], zf),
        go(gp2.at[ring(z, -d)], rpz.at[2], zb),
    ]
    for i in range(2):
        qz3[i].wait_recv()
        qz2[i].wait_recv()
        own = add(gq[z, i], rqz[1, i], rqz[2, i])
        for yh_ in range(2):
            cut = own[yh_ * HALF : (yh_ + 1) * HALF]
            own_q2[i, yh_] = cut
            gq2[i, yh_] = cut.astype(BF)

    def q2(ref, y_):
        return ref.at[(y_ + y) % 2, y_ // 2]

    qy = [
        go(q2(gq2, ring(y, 2)), rqy.at[0], y2),
        go(q2(gq2, ring(y, d)), rqy.at[1], yf),
        go(q2(gq2, ring(y, -d)), rqy.at[2], yb),
    ]
    for copy in pz:
        copy.wait_recv()
    res_img[0:HALF, :] = (own_p2[z] + add(rpz[0], rpz[1], rpz[2])).astype(BF)
    for copy in qy:
        copy.wait_recv()
    res_img[HALF:IMG, :] = (own_q2[0, yh] + add(rqy[0], rqy[1], rqy[2])).astype(BF)
    store_img = load(5, res_img, out_img)
    for copy in copies:
        copy.wait_send()
    store_cap.wait()
    store_img.wait()


def finish(img, cap, out_img, out_cap):
    out_img[...] = img[...]
    out_cap[...] = cap[...]


COPIES = 96


def body(pic, sent, wp, ws, counts, sharp, bias):
    vm = pl.BlockSpec(memory_space=pltpu.VMEM)
    sm = pl.BlockSpec(memory_space=pltpu.SMEM)
    hbm = pl.BlockSpec(memory_space=pl.ANY)
    scratch = [
        ((IMG, D), BF),
        ((4 * CAP, D), BF),
        ((D, D), BF),
        ((D, D), BF),
        ((4 * PAD, D), BF),
        ((4 * CAP, D), BF),
        ((2, 4 * CAP, 2 * PAD), BF),
        ((2, 8, 2 * PAD), F32),
        ((2, 48, 128), F32),
        ((4, CAP, D), BF),
        ((CAP, D), F32),
        ((CAP, D), F32),
        ((3, CAP, D), BF),
        ((CAP, D), BF),
        ((2, IMG, D), BF),
        ((2, IMG, D), F32),
        ((2, IMG, D), BF),
        ((2, HALF, D), BF),
        ((4, 2, 2 * HALF, SL), BF),
        ((3, HALF, 512), BF),
        ((HALF, 512), BF),
        ((4, HALF, SL), BF),
        ((4, HALF, SL), F32),
        ((3, HALF, SL), BF),
        ((3, 2, 2 * HALF, SL), BF),
        ((2, 2 * HALF, SL), BF),
        ((2, 2, HALF, SL), BF),
        ((2, 2, HALF, SL), F32),
        ((3, HALF, SL), BF),
        ((IMG, SL), BF),
        ((CAP, D), BF),
    ]
    outs = (
        jax.ShapeDtypeStruct((IMG, SL), BF),
        jax.ShapeDtypeStruct((CAP, D), BF),
    )
    img, cap = pl.pallas_call(
        kernel,
        out_shape=outs,
        in_specs=[hbm] * 4 + [vm] + [sm] * 2,
        out_specs=(hbm, hbm),
        scratch_shapes=[pltpu.VMEM(shape, kind) for shape, kind in scratch]
        + [
            pltpu.SemaphoreType.DMA((COPIES,)),
            pltpu.SemaphoreType.DMA((COPIES,)),
            pltpu.SemaphoreType.DMA((6,)),
        ],
        compiler_params=pltpu.CompilerParams(
            collective_id=0, has_side_effects=True, vmem_limit_bytes=58 * 1024 * 1024
        ),
    )(pic, sent, wp, ws, counts.reshape(44, 128), sharp, bias)
    return pl.pallas_call(
        finish, out_shape=outs, in_specs=[vm, vm], out_specs=(vm, vm)
    )(img, cap)


def solution(mesh):
    in_specs = (
        P("dp", None),
        P(("dp", "tensor"), None),
        P(None, "tensor"),
        P(None, "tensor"),
        P(),
        P(),
        P(),
    )
    out_specs = (P("dp", "tensor"), P(("dp", "tensor"), None))
    return jax.shard_map(body, mesh=mesh, in_specs=in_specs, out_specs=out_specs, check_vma=False)
```

```python
import jax
import jax.numpy as jnp
from jax import lax
from jax.experimental import pallas as pl
from jax.experimental.pallas import tpu as pltpu
from jax.sharding import PartitionSpec as P

EPS = 1e-06
LOG2E = 1.4426950408889634
MESH = pl.DeviceIdType.MESH
BF = jnp.bfloat16
F32 = jnp.float32

D = 1024
IMG = 352
PAD = 384
HALF = 176
CUT = 256
CAP = 176
SL = 128
NT = (((1,), (1,)), ((), ()))
TN = (((0,), (0,)), ((), ()))


def mo(v, k):
    return pl.multiple_of(v, k)


def kernel(
    pic,
    sent,
    wp,
    ws,
    counts,
    sharp,
    bias,
    out_img,
    out_cap,
    pic_v,
    wp_v,
    feat,
    wcap,
    wimg,
    plane,
    caps,
    coef,
    vecs,
    starts,
    part,
    own_cap,
    raw_cap,
    cap_in,
    cap_mid,
    img_send,
    img_own,
    img_recv,
    gp,
    gq,
    rpy,
    tpy,
    gp2,
    own_p2,
    rpz,
    rqz,
    tqz,
    gq2,
    own_q2,
    rqy,
    res_img,
    res_cap,
    send_sem,
    recv_sem,
    load_sem,
):
    dp = lax.axis_index("dp")
    tensor = lax.axis_index("tensor")
    c = dp % 2
    x = (dp // 2) % 4
    yl = dp // 8
    yh = tensor // 4
    z = tensor % 4
    y = yh * 2 + yl
    d = 1 - 2 * c

    def dev(x_, y_, z_, c_):
        return ((y_ % 2) * 8 + x_ * 2 + c_, (y_ // 2) * 4 + z_)

    def ring(v, s):
        return (v + 4 + s) % 4

    def col(yh_, z_):
        return pl.ds(mo((yh_ * 4 + z_) * SL, SL), SL)

    x2 = dev(ring(x, 2), y, z, c)
    xf, xb = dev(ring(x, d), y, z, c), dev(ring(x, -d), y, z, c)
    yf, yb = dev(x, ring(y, d), z, c), dev(x, ring(y, -d), z, c)
    y2 = dev(x, ring(y, 2), z, c)
    zf, zb = dev(x, y, ring(z, d), c), dev(x, y, ring(z, -d), c)
    z2 = dev(x, y, ring(z, 2), c)
    core = dev(x, y, z, 1 - c)
    ym = dev(x, 3 - y, z, c)

    barrier = pltpu.get_barrier_semaphore()
    for other in (xf, xb, x2, yf, yb, y2, zf, zb, z2, core):
        pl.semaphore_signal(barrier, inc=1, device_id=other, device_id_type=MESH)

    def load(i, src, dst):
        copy = pltpu.make_async_copy(src, dst, load_sem.at[i])
        copy.start()
        return copy

    load_pic = load(0, pic, pic_v)
    load_wp = load(1, wp, wp_v)
    load_ws = load(2, ws, wcap.at[:, col(yh, z)])
    load_sent = load(3, sent, feat.at[3 * CAP : 4 * CAP])

    copies = []

    def make(src, dst, target):
        i = len(copies)
        copy = pltpu.make_async_remote_copy(
            src_ref=src,
            dst_ref=dst,
            send_sem=send_sem.at[i],
            recv_sem=recv_sem.at[i],
            device_id=target,
            device_id_type=MESH,
        )
        copies.append(copy)
        return copy

    def go(src, dst, target):
        copy = make(src, dst, target)
        copy.start()
        return copy

    def head_rows(x_):
        return pl.ds(mo((x_ * 2 + c) * 128, 128), 128)

    k_own = yl * 2 + c
    zero = jnp.zeros((PAD - IMG, D), BF)
    for k in range(4):
        plane[k * PAD + IMG : (k + 1) * PAD, :] = zero
    load_wp.wait()
    load_pic.wait()
    plane[pl.ds(mo(k_own * PAD, PAD), IMG), col(yh, z)] = jnp.dot(
        pic_v[...], wp_v[...], preferred_element_type=F32
    ).astype(BF)
    wimg[head_rows(x), col(yh, z)] = wp_v[head_rows(x), :]
    pl.semaphore_wait(barrier, 10)

    def p_rows(y_, lo=0, num=CUT):
        return pl.ds(mo(((y_ % 2) * 2 + c) * PAD + lo, 16), num)

    def q_rows(y_):
        return pl.ds(mo(((y_ % 2) * 2 + c) * PAD + CUT, 16), IMG - CUT)

    def p_z(z_, target):
        ref = plane.at[p_rows(y), col(yh, z_)]
        return go(ref, ref, target)

    def p_y(y_, target, lo=0, num=CUT):
        ref = plane.at[p_rows(y_, lo, num), pl.ds(mo((y_ // 2) * 512, 512), 512)]
        return go(ref, ref, target)

    def q_y(y_, target):
        ref = plane.at[q_rows(y_), col(y_ // 2, z)]
        return go(ref, ref, target)

    def q_z(z_, target):
        made = []
        for y_ in range(4):
            ref = plane.at[q_rows(y_), col(y_ // 2, z_)]
            made.append(go(ref, ref, target))
        return made

    hc = mo(c * 512, 512)

    half = ws.at[pl.ds(hc, 512)]
    here = wcap.at[pl.ds(hc, 512), col(yh, z)]

    def same(yh_, z_, target):
        ref = wcap.at[pl.ds(hc, 512), col(yh_, z_)]
        return go(ref, ref, target)

    def few(yh_, target):
        ref = wimg.at[head_rows(x), col(yh_, z)]
        return go(ref, ref, target)

    def many(x_, target, start=True):
        ref = wimg.at[head_rows(x_)]
        return (go if start else make)(ref, ref, target)

    def slot_rows(slot, lo, hi):
        return feat.at[slot * CAP + lo : slot * CAP + hi]

    ihead = [few(yh, target) for target in (ym, zf, zb, z2)]
    pz = [p_z(z, target) for target in (zf, zb, z2)]
    qy = [q_y(y, target) for target in (yf, yb, y2)]
    head = {"m": go(half, here, ym), "f": go(half, here, zf), "b": go(half, here, zb)}
    xf1 = go(sent.at[0:96], slot_rows(1, 0, 96), xf)
    xb1 = go(sent, slot_rows(2, 0, CAP), xb)
    xf2 = go(sent.at[96:CAP], slot_rows(1, 96, CAP), xf)

    for copy in qy:
        copy.wait_recv()
    qzf, qzb = q_z(z, zf), q_z(z, zb)
    ihead[0].wait_recv()
    ihead += [few(1 - yh, target) for target in (zf, zb, z2)]
    for copy in pz:
        copy.wait_recv()
    pyf0 = p_y(y, yf, 0, CUT // 2)
    pyb = p_y(y, yb)
    pyf1 = p_y(y, yf, CUT // 2, CUT // 2)
    swaps = [p_y(y, core)]
    head["m"].wait_recv()
    head_mf = same(1 - yh, z, zf)
    head_mb = same(1 - yh, z, zb)
    cores = [same(1 - yh, z, core)]
    head["f"].wait_recv()
    head_ff = same(yh, ring(z, -d), zf)
    cores.append(same(yh, ring(z, -d), core))
    xf1.wait_recv()
    xff1 = go(slot_rows(1, 0, 96), slot_rows(0, 0, 96), xf)
    pyf0.wait_recv()
    pyff0 = p_y(ring(y, -d), yf, 0, CUT // 2)
    head["b"].wait_recv()
    cores.append(same(yh, ring(z, d), core))
    for copy in qzf:
        copy.wait_recv()
    qzff = q_z(ring(z, -d), zf)
    head_mf.wait_recv()
    head_mff = same(1 - yh, ring(z, -d), zf)
    cores.append(same(1 - yh, ring(z, -d), core))
    xf2.wait_recv()
    xff2 = go(slot_rows(1, 96, CAP), slot_rows(0, 96, CAP), xf)
    for copy in ihead[1:]:
        copy.wait_recv()
    icores = [many(x, core)]
    icores += [many(ring(x, step), core, False) for step in (-d, d, 2)]
    iway = [many(x, target) for target in (xf, xb, x2)]
    pyf1.wait_recv()
    pyff1 = p_y(ring(y, -d), yf, CUT // 2, CUT // 2)
    swaps.append(p_y(ring(y, -d), core))

    n = counts[...].astype(F32)
    nb = n.astype(BF)
    a = lax.broadcasted_iota(jnp.int32, (128, 128), 0)
    b = lax.broadcasted_iota(jnp.int32, (128, 128), 1)
    upto = jnp.dot(nb, (a < b).astype(F32).astype(BF), preferred_element_type=F32)
    a = lax.broadcasted_iota(jnp.int32, (44, 44), 0)
    b = lax.broadcasted_iota(jnp.int32, (44, 44), 1)
    before = jnp.dot((b < a).astype(F32).astype(BF), nb, preferred_element_type=F32)
    starts[0, 0:44, :] = upto + jnp.sum(before, axis=1, keepdims=True)
    starts[1, 0:44, :] = n
    starts[0, 44:48, :] = jnp.full((4, 128), -1.0, F32)
    starts[1, 44:48, :] = jnp.full((4, 128), 1.0, F32)

    head_ff.wait_recv()
    cores.append(same(yh, ring(z, 2), core))
    head_mb.wait_recv()
    cores.append(same(1 - yh, ring(z, d), core))
    pyb.wait_recv()
    swaps.append(p_y(ring(y, d), core))
    head_mff.wait_recv()
    cores.append(same(1 - yh, ring(z, 2), core))
    for copy in cores:
        copy.wait_recv()

    load_ws.wait()
    load_sent.wait()

    def embed(rows):
        raw = jnp.dot(feat[rows, :], wcap[...], preferred_element_type=F32)
        cap_scale = lax.rsqrt(jnp.sum(raw * raw, axis=1, keepdims=True) + EPS)
        caps[rows, :] = (raw * cap_scale).astype(BF)
        return raw

    xb1.wait_recv()
    raw_cap[...] = embed(slice(2 * CAP, 4 * CAP))[CAP : 2 * CAP]
    pyff0.wait_recv()
    pyff1.wait_recv()
    swaps.append(p_y(ring(y, 2), core))
    for copy in qzb + qzff:
        copy.wait_recv()
    for yl_ in range(2):
        ref = plane.at[q_rows(yl_)]
        swaps.append(go(ref, ref, core))
    xff1.wait_recv()
    xff2.wait_recv()
    embed(slice(0, 2 * CAP))
    for copy in swaps:
        copy.wait_recv()

    t = sharp[0]
    shift = bias[0] * LOG2E
    ones = jnp.ones((8, D), BF)
    even = x % 2 == 0

    def block_vec(which, yl_, c_):
        row = (yl_ * 4 + x) * 2 + c_
        q = (row * 11) // 4
        v = jnp.concatenate([starts[which, pl.ds(q + i, 1), :] for i in range(4)], axis=1)
        cuts = [((2 * p + 3 * c_) % 4) * 32 for p in range(2)]
        return jnp.where(even, v[:, cuts[0] : cuts[0] + PAD], v[:, cuts[1] : cuts[1] + PAD])

    for yl_ in range(2):
        for c_ in range(2):
            k = yl_ * 2 + c_
            zk = plane[k * PAD : (k + 1) * PAD, :]
            square = lax.dot_general(ones, zk * zk, NT, preferred_element_type=F32)
            scale = t * lax.rsqrt(square[0:1, :] + EPS)
            first = block_vec(0, yl_, c_)
            num = block_vec(1, yl_, c_)
            lanes = slice(c_ * PAD, (c_ + 1) * PAD)
            vecs[yl_, 0:1, lanes] = scale * LOG2E
            vecs[yl_, 1:2, lanes] = scale
            vecs[yl_, 2:3, lanes] = -scale / num
            vecs[yl_, 3:4, lanes] = first
            vecs[yl_, 4:5, lanes] = first + num

    t1 = make(part.at[0], cap_in.at[0], xf)
    t3 = make(part.at[1], cap_in.at[2], xb)

    def base(step):
        return (((yl * 4 + ring(x, step)) * 2 + c) * 8 + tensor) * CAP

    def two_slots(g, carry):
        low = jnp.where(g == 0, base(2), base(d))
        high = jnp.where(g == 0, base(-d), base(0))
        i = lax.broadcasted_iota(jnp.int32, (2 * CAP, 1), 0)
        number = (i + jnp.where(i < CAP, low, high - CAP)).astype(F32)
        r = pl.ds(mo(g * 2 * CAP, 2 * CAP), 2 * CAP)
        total = None
        for yl_ in range(2):
            zy = plane[yl_ * 2 * PAD : (yl_ + 1) * 2 * PAD, :]
            s = lax.dot_general(caps[r, :], zy, NT, preferred_element_type=F32)
            l2 = s * vecs[yl_, 0:1, :] + shift
            inside = (number >= vecs[yl_, 3:4, :]) & (number < vecs[yl_, 4:5, :])
            e = jnp.exp2(jnp.where(inside, l2, -l2))
            w = jnp.where(inside, vecs[yl_, 2:3, :], vecs[yl_, 1:2, :])
            f = (w / (1.0 + e)).astype(BF)
            coef[yl_, r, :] = f
            more = jnp.dot(f, zy, preferred_element_type=F32)
            total = more if total is None else total + more
        part[2 * g] = total[0:CAP].astype(BF)
        part[2 * g + 1] = total[CAP : 2 * CAP].astype(BF)

        @pl.when(g == 0)
        def _():
            t1.start()

        @pl.when(g == 1)
        def _():
            own_cap[...] = total[CAP : 2 * CAP]
            t3.start()
            for arrived, copy in zip(iway[0:2], icores[1:3]):
                arrived.wait_recv()
                copy.start()

        return carry

    lax.fori_loop(0, 2, two_slots, 0)

    def grad_rows(yl_, c_):
        f = coef[yl_, :, pl.ds(mo(c_ * PAD, PAD), PAD)]
        return lax.dot_general(f, caps[...], TN, preferred_element_type=F32)

    given = []
    for i, yl_ in enumerate((yl, 1 - yl)):
        img_send[i] = grad_rows(yl_, 1 - c)[0:IMG].astype(BF)
        given.append(go(img_send.at[i], img_recv.at[i], core))
        if i == 0:
            img_own[0] = grad_rows(yl_, c)[0:IMG]
    iway[2].wait_recv()
    icores[3].start()
    for copy in icores:
        copy.wait_recv()

    def gp_part(y_):
        return gp.at[y_ % 2, :, pl.ds(mo((y_ // 2) * 512, 512), 512)]

    def image_back(i, yl_):
        given[i].wait_recv()
        g = img_own[i] + img_recv[i].astype(F32)
        u = plane[pl.ds(mo((yl_ * 2 + c) * PAD, PAD), IMG), :].astype(F32)
        size = jnp.sum(u * u, axis=1, keepdims=True) + EPS
        along = jnp.sum(u * g, axis=1, keepdims=True)
        back = (g - u * (along / size)).astype(BF)
        grad = lax.dot_general(back, wimg[...], NT, preferred_element_type=F32)
        gp[yl_] = grad[0:HALF].astype(BF)
        for z_ in range(4):
            for yh_ in range(2):
                j = yh_ * 4 + z_
                gq[z_, i, yh_ * HALF : (yh_ + 1) * HALF, :] = grad[
                    HALF:IMG, j * SL : (j + 1) * SL
                ].astype(BF)

    def add(*refs):
        total = refs[0].astype(F32)
        for ref in refs[1:]:
            total = total + ref.astype(F32)
        return total

    image_back(0, yl)
    py1 = go(gp_part(ring(y, 2)), rpy.at[0], yf)
    qz1 = [go(gq.at[ring(z, 2), 0], rqz.at[0, 0], zf)]
    qz3 = [go(gq.at[ring(z, -d), 0], rqz.at[2, 0], zb)]
    img_own[1] = grad_rows(1 - yl, c)[0:IMG]
    t1.wait_recv()
    cap_mid[...] = (part[2].astype(F32) + cap_in[0].astype(F32)).astype(BF)
    t2 = go(cap_mid, cap_in.at[1], xf)
    image_back(1, 1 - yl)
    py3 = go(gp_part(ring(y, -d)), rpy.at[2], yb)
    qz1.append(go(gq.at[ring(z, 2), 1], rqz.at[0, 1], zf))
    qz3.append(go(gq.at[ring(z, -d), 1], rqz.at[2, 1], zb))
    py1.wait_recv()
    tpy[...] = add(gp_part(ring(y, d))[...], rpy[0]).astype(BF)
    py2 = go(tpy, rpy.at[1], yf)
    qz2 = []
    for i in range(2):
        qz1[i].wait_recv()
        tqz[i] = add(gq[ring(z, d), i], rqz[0, i]).astype(BF)
        qz2.append(go(tqz.at[i], rqz.at[1, i], zf))

    t2.wait_recv()
    t3.wait_recv()
    g = own_cap[...] + cap_in[1].astype(F32) + cap_in[2].astype(F32)
    raw = raw_cap[...]
    cap_scale = lax.rsqrt(jnp.sum(raw * raw, axis=1, keepdims=True) + EPS)
    u = raw * cap_scale
    along = jnp.sum(u * g, axis=1, keepdims=True)
    back = (cap_scale * (g - u * along)).astype(BF)
    res_cap[...] = lax.dot_general(
        back, wcap[...], NT, preferred_element_type=F32
    ).astype(BF)
    store_cap = load(4, res_cap, out_cap)

    py3.wait_recv()
    py2.wait_recv()
    own = add(gp_part(y)[...], rpy[1], rpy[2])
    for z_ in range(4):
        cut = own[:, z_ * SL : (z_ + 1) * SL]
        own_p2[z_] = cut
        gp2[z_] = cut.astype(BF)
    pz = [
        go(gp2.at[ring(z, 2)], rpz.at[0], z2),
        go(gp2.at[ring(z, d)], rpz.at[1], zf),
        go(gp2.at[ring(z, -d)], rpz.at[2], zb),
    ]
    for i in range(2):
        qz3[i].wait_recv()
        qz2[i].wait_recv()
        own = add(gq[z, i], rqz[1, i], rqz[2, i])
        for yh_ in range(2):
            cut = own[yh_ * HALF : (yh_ + 1) * HALF]
            own_q2[i, yh_] = cut
            gq2[i, yh_] = cut.astype(BF)

    def q2(ref, y_):
        return ref.at[(y_ + y) % 2, y_ // 2]

    qy = [
        go(q2(gq2, ring(y, 2)), rqy.at[0], y2),
        go(q2(gq2, ring(y, d)), rqy.at[1], yf),
        go(q2(gq2, ring(y, -d)), rqy.at[2], yb),
    ]
    for copy in pz:
        copy.wait_recv()
    res_img[0:HALF, :] = (own_p2[z] + add(rpz[0], rpz[1], rpz[2])).astype(BF)
    for copy in qy:
        copy.wait_recv()
    res_img[HALF:IMG, :] = (own_q2[0, yh] + add(rqy[0], rqy[1], rqy[2])).astype(BF)
    store_img = load(5, res_img, out_img)
    for copy in copies:
        copy.wait_send()
    store_cap.wait()
    store_img.wait()


def finish(img, cap, out_img, out_cap):
    out_img[...] = img[...]
    out_cap[...] = cap[...]


COPIES = 96


def body(pic, sent, wp, ws, counts, sharp, bias):
    vm = pl.BlockSpec(memory_space=pltpu.VMEM)
    sm = pl.BlockSpec(memory_space=pltpu.SMEM)
    hbm = pl.BlockSpec(memory_space=pl.ANY)
    scratch = [
        ((IMG, D), BF),
        ((D, SL), BF),
        ((4 * CAP, D), BF),
        ((D, D), BF),
        ((D, D), BF),
        ((4 * PAD, D), BF),
        ((4 * CAP, D), BF),
        ((2, 4 * CAP, 2 * PAD), BF),
        ((2, 8, 2 * PAD), F32),
        ((2, 48, 128), F32),
        ((4, CAP, D), BF),
        ((CAP, D), F32),
        ((CAP, D), F32),
        ((3, CAP, D), BF),
        ((CAP, D), BF),
        ((2, IMG, D), BF),
        ((2, IMG, D), F32),
        ((2, IMG, D), BF),
        ((2, HALF, D), BF),
        ((4, 2, 2 * HALF, SL), BF),
        ((3, HALF, 512), BF),
        ((HALF, 512), BF),
        ((4, HALF, SL), BF),
        ((4, HALF, SL), F32),
        ((3, HALF, SL), BF),
        ((3, 2, 2 * HALF, SL), BF),
        ((2, 2 * HALF, SL), BF),
        ((2, 2, HALF, SL), BF),
        ((2, 2, HALF, SL), F32),
        ((3, HALF, SL), BF),
        ((IMG, SL), BF),
        ((CAP, D), BF),
    ]
    outs = (
        jax.ShapeDtypeStruct((IMG, SL), BF),
        jax.ShapeDtypeStruct((CAP, D), BF),
    )
    img, cap = pl.pallas_call(
        kernel,
        out_shape=outs,
        in_specs=[hbm] * 4 + [vm] + [sm] * 2,
        out_specs=(hbm, hbm),
        scratch_shapes=[pltpu.VMEM(shape, kind) for shape, kind in scratch]
        + [
            pltpu.SemaphoreType.DMA((COPIES,)),
            pltpu.SemaphoreType.DMA((COPIES,)),
            pltpu.SemaphoreType.DMA((6,)),
        ],
        compiler_params=pltpu.CompilerParams(
            collective_id=0, has_side_effects=True, vmem_limit_bytes=58 * 1024 * 1024
        ),
    )(pic, sent, wp, ws, counts.reshape(44, 128), sharp, bias)
    return pl.pallas_call(
        finish, out_shape=outs, in_specs=[vm, vm], out_specs=(vm, vm)
    )(img, cap)


def solution(mesh):
    in_specs = (
        P("dp", None),
        P(("dp", "tensor"), None),
        P(None, "tensor"),
        P(None, "tensor"),
        P(),
        P(),
        P(),
    )
    out_specs = (P("dp", "tensor"), P(("dp", "tensor"), None))
    return jax.shard_map(body, mesh=mesh, in_specs=in_specs, out_specs=out_specs, check_vma=False)
```

```python
import jax
import jax.numpy as jnp
from jax import lax
from jax.experimental import pallas as pl
from jax.experimental.pallas import tpu as pltpu
from jax.sharding import PartitionSpec as P

EPS = 1e-06
LOG2E = 1.4426950408889634
MESH = pl.DeviceIdType.MESH
BF = jnp.bfloat16
F32 = jnp.float32

D = 1024
IMG = 352
PAD = 384
HALF = 176
CUT = 256
CAP = 176
SL = 128
NT = (((1,), (1,)), ((), ()))
TN = (((0,), (0,)), ((), ()))


def mo(v, k):
    return pl.multiple_of(v, k)


def kernel(
    pic,
    sent,
    wp,
    ws,
    counts,
    sharp,
    bias,
    out_img,
    out_cap,
    pic_v,
    wp_v,
    feat,
    wcap,
    wimg,
    plane,
    caps,
    coef,
    vecs,
    starts,
    part,
    own_cap,
    raw_cap,
    cap_in,
    cap_mid,
    img_send,
    img_own,
    img_recv,
    gp,
    gq,
    rpy,
    tpy,
    gp2,
    own_p2,
    rpz,
    rqz,
    gq2,
    own_q2,
    rqy,
    res_img,
    res_cap,
    send_sem,
    recv_sem,
    load_sem,
):
    dp = lax.axis_index("dp")
    tensor = lax.axis_index("tensor")
    c = dp % 2
    x = (dp // 2) % 4
    yl = dp // 8
    yh = tensor // 4
    z = tensor % 4
    y = yh * 2 + yl
    d = 1 - 2 * c

    def dev(x_, y_, z_, c_):
        return ((y_ % 2) * 8 + x_ * 2 + c_, (y_ // 2) * 4 + z_)

    def ring(v, s):
        return (v + 4 + s) % 4

    def col(yh_, z_):
        return pl.ds(mo((yh_ * 4 + z_) * SL, SL), SL)

    x2 = dev(ring(x, 2), y, z, c)
    xf, xb = dev(ring(x, d), y, z, c), dev(ring(x, -d), y, z, c)
    yf, yb = dev(x, ring(y, d), z, c), dev(x, ring(y, -d), z, c)
    y2 = dev(x, ring(y, 2), z, c)
    zf, zb = dev(x, y, ring(z, d), c), dev(x, y, ring(z, -d), c)
    z2 = dev(x, y, ring(z, 2), c)
    core = dev(x, y, z, 1 - c)
    ym = dev(x, 3 - y, z, c)

    barrier = pltpu.get_barrier_semaphore()
    for other in (xf, xb, x2, yf, yb, y2, zf, zb, z2, core):
        pl.semaphore_signal(barrier, inc=1, device_id=other, device_id_type=MESH)

    def load(i, src, dst):
        copy = pltpu.make_async_copy(src, dst, load_sem.at[i])
        copy.start()
        return copy

    load_pic = load(0, pic, pic_v)
    load_wp = load(1, wp, wp_v)
    load_ws = load(2, ws, wcap.at[:, col(yh, z)])
    load_sent = load(3, sent, feat.at[3 * CAP : 4 * CAP])

    copies = []

    def make(src, dst, target):
        i = len(copies)
        copy = pltpu.make_async_remote_copy(
            src_ref=src,
            dst_ref=dst,
            send_sem=send_sem.at[i],
            recv_sem=recv_sem.at[i],
            device_id=target,
            device_id_type=MESH,
        )
        copies.append(copy)
        return copy

    def go(src, dst, target):
        copy = make(src, dst, target)
        copy.start()
        return copy

    def head_rows(x_):
        return pl.ds(mo((x_ * 2 + c) * 128, 128), 128)

    k_own = yl * 2 + c
    zero = jnp.zeros((PAD - IMG, D), BF)
    for k in range(4):
        plane[k * PAD + IMG : (k + 1) * PAD, :] = zero
    load_wp.wait()
    load_pic.wait()
    plane[pl.ds(mo(k_own * PAD, PAD), IMG), col(yh, z)] = jnp.dot(
        pic_v[...], wp_v[...], preferred_element_type=F32
    ).astype(BF)
    wimg[head_rows(x), col(yh, z)] = wp_v[head_rows(x), :]
    pl.semaphore_wait(barrier, 10)

    def p_rows(y_, lo=0, num=CUT):
        return pl.ds(mo(((y_ % 2) * 2 + c) * PAD + lo, 16), num)

    def q_rows(y_):
        return pl.ds(mo(((y_ % 2) * 2 + c) * PAD + CUT, 16), IMG - CUT)

    def p_z(z_, target):
        ref = plane.at[p_rows(y), col(yh, z_)]
        return go(ref, ref, target)

    def p_y(y_, target, lo=0, num=CUT):
        ref = plane.at[p_rows(y_, lo, num), pl.ds(mo((y_ // 2) * 512, 512), 512)]
        return go(ref, ref, target)

    def q_y(y_, target):
        ref = plane.at[q_rows(y_), col(y_ // 2, z)]
        return go(ref, ref, target)

    def q_z(z_, target):
        made = []
        for y_ in range(4):
            ref = plane.at[q_rows(y_), col(y_ // 2, z_)]
            made.append(go(ref, ref, target))
        return made

    hc = mo(c * 512, 512)

    half = ws.at[pl.ds(hc, 512)]
    here = wcap.at[pl.ds(hc, 512), col(yh, z)]

    def same(yh_, z_, target):
        ref = wcap.at[pl.ds(hc, 512), col(yh_, z_)]
        return go(ref, ref, target)

    def few(yh_, target):
        ref = wimg.at[head_rows(x), col(yh_, z)]
        return go(ref, ref, target)

    def many(x_, target, start=True):
        ref = wimg.at[head_rows(x_)]
        return (go if start else make)(ref, ref, target)

    def slot_rows(slot, lo, hi):
        return feat.at[slot * CAP + lo : slot * CAP + hi]

    ihead = [few(yh, target) for target in (ym, zf, zb, z2)]
    pz = [p_z(z, target) for target in (zf, zb, z2)]
    qy = [q_y(y, target) for target in (yf, yb, y2)]
    head = {"m": go(half, here, ym), "f": go(half, here, zf), "b": go(half, here, zb)}
    xf1 = go(sent.at[0:96], slot_rows(1, 0, 96), xf)
    xb1 = go(sent, slot_rows(2, 0, CAP), xb)
    xf2 = go(sent.at[96:CAP], slot_rows(1, 96, CAP), xf)

    for copy in qy:
        copy.wait_recv()
    qzf, qzb = q_z(z, zf), q_z(z, zb)
    ihead[0].wait_recv()
    ihead += [few(1 - yh, target) for target in (zf, zb, z2)]
    for copy in pz:
        copy.wait_recv()
    pyf0 = p_y(y, yf, 0, CUT // 2)
    pyb = p_y(y, yb)
    pyf1 = p_y(y, yf, CUT // 2, CUT // 2)
    swaps = [p_y(y, core)]
    head["m"].wait_recv()
    head_mf = same(1 - yh, z, zf)
    head_mb = same(1 - yh, z, zb)
    cores = [same(1 - yh, z, core)]
    head["f"].wait_recv()
    head_ff = same(yh, ring(z, -d), zf)
    cores.append(same(yh, ring(z, -d), core))
    xf1.wait_recv()
    xff1 = go(slot_rows(1, 0, 96), slot_rows(0, 0, 96), xf)
    pyf0.wait_recv()
    pyff0 = p_y(ring(y, -d), yf, 0, CUT // 2)
    head["b"].wait_recv()
    cores.append(same(yh, ring(z, d), core))
    for copy in qzf:
        copy.wait_recv()
    qzff = q_z(ring(z, -d), zf)
    head_mf.wait_recv()
    head_mff = same(1 - yh, ring(z, -d), zf)
    cores.append(same(1 - yh, ring(z, -d), core))
    xf2.wait_recv()
    xff2 = go(slot_rows(1, 96, CAP), slot_rows(0, 96, CAP), xf)
    for copy in ihead[1:]:
        copy.wait_recv()
    icores = [many(x, core)]
    icores += [many(ring(x, step), core, False) for step in (-d, d, 2)]
    iway = [many(x, target) for target in (xf, xb, x2)]
    pyf1.wait_recv()
    pyff1 = p_y(ring(y, -d), yf, CUT // 2, CUT // 2)
    swaps.append(p_y(ring(y, -d), core))

    n = counts[...].astype(F32)
    nb = n.astype(BF)
    a = lax.broadcasted_iota(jnp.int32, (128, 128), 0)
    b = lax.broadcasted_iota(jnp.int32, (128, 128), 1)
    upto = jnp.dot(nb, (a < b).astype(F32).astype(BF), preferred_element_type=F32)
    a = lax.broadcasted_iota(jnp.int32, (44, 44), 0)
    b = lax.broadcasted_iota(jnp.int32, (44, 44), 1)
    before = jnp.dot((b < a).astype(F32).astype(BF), nb, preferred_element_type=F32)
    starts[0, 0:44, :] = upto + jnp.sum(before, axis=1, keepdims=True)
    starts[1, 0:44, :] = n
    starts[0, 44:48, :] = jnp.full((4, 128), -1.0, F32)
    starts[1, 44:48, :] = jnp.full((4, 128), 1.0, F32)

    head_ff.wait_recv()
    cores.append(same(yh, ring(z, 2), core))
    head_mb.wait_recv()
    cores.append(same(1 - yh, ring(z, d), core))
    pyb.wait_recv()
    swaps.append(p_y(ring(y, d), core))
    head_mff.wait_recv()
    cores.append(same(1 - yh, ring(z, 2), core))
    for copy in cores:
        copy.wait_recv()

    load_ws.wait()
    load_sent.wait()

    def embed(rows):
        raw = jnp.dot(feat[rows, :], wcap[...], preferred_element_type=F32)
        cap_scale = lax.rsqrt(jnp.sum(raw * raw, axis=1, keepdims=True) + EPS)
        caps[rows, :] = (raw * cap_scale).astype(BF)
        return raw

    xb1.wait_recv()
    raw_cap[...] = embed(slice(2 * CAP, 4 * CAP))[CAP : 2 * CAP]
    pyff0.wait_recv()
    pyff1.wait_recv()
    swaps.append(p_y(ring(y, 2), core))
    for copy in qzb + qzff:
        copy.wait_recv()
    for yl_ in range(2):
        ref = plane.at[q_rows(yl_)]
        swaps.append(go(ref, ref, core))
    xff1.wait_recv()
    xff2.wait_recv()
    embed(slice(0, 2 * CAP))
    for copy in swaps:
        copy.wait_recv()

    t = sharp[0]
    shift = bias[0] * LOG2E
    ones = jnp.ones((8, D), BF)
    even = x % 2 == 0

    def block_vec(which, yl_, c_):
        row = (yl_ * 4 + x) * 2 + c_
        q = (row * 11) // 4
        v = jnp.concatenate([starts[which, pl.ds(q + i, 1), :] for i in range(4)], axis=1)
        cuts = [((2 * p + 3 * c_) % 4) * 32 for p in range(2)]
        return jnp.where(even, v[:, cuts[0] : cuts[0] + PAD], v[:, cuts[1] : cuts[1] + PAD])

    for yl_ in range(2):
        for c_ in range(2):
            k = yl_ * 2 + c_
            zk = plane[k * PAD : (k + 1) * PAD, :]
            square = lax.dot_general(ones, zk * zk, NT, preferred_element_type=F32)
            scale = t * lax.rsqrt(square[0:1, :] + EPS)
            first = block_vec(0, yl_, c_)
            num = block_vec(1, yl_, c_)
            lanes = slice(c_ * PAD, (c_ + 1) * PAD)
            vecs[yl_, 0:1, lanes] = scale * LOG2E
            vecs[yl_, 1:2, lanes] = scale
            vecs[yl_, 2:3, lanes] = -scale / num
            vecs[yl_, 3:4, lanes] = first
            vecs[yl_, 4:5, lanes] = first + num

    t1 = make(part.at[0], cap_in.at[0], xf)
    t3 = make(part.at[1], cap_in.at[2], xb)

    def base(step):
        return (((yl * 4 + ring(x, step)) * 2 + c) * 8 + tensor) * CAP

    def two_slots(g, carry):
        low = jnp.where(g == 0, base(2), base(d))
        high = jnp.where(g == 0, base(-d), base(0))
        i = lax.broadcasted_iota(jnp.int32, (2 * CAP, 1), 0)
        number = (i + jnp.where(i < CAP, low, high - CAP)).astype(F32)
        r = pl.ds(mo(g * 2 * CAP, 2 * CAP), 2 * CAP)
        total = None
        for yl_ in range(2):
            zy = plane[yl_ * 2 * PAD : (yl_ + 1) * 2 * PAD, :]
            s = lax.dot_general(caps[r, :], zy, NT, preferred_element_type=F32)
            l2 = s * vecs[yl_, 0:1, :] + shift
            inside = (number >= vecs[yl_, 3:4, :]) & (number < vecs[yl_, 4:5, :])
            e = jnp.exp2(jnp.where(inside, l2, -l2))
            w = jnp.where(inside, vecs[yl_, 2:3, :], vecs[yl_, 1:2, :])
            f = (w / (1.0 + e)).astype(BF)
            coef[yl_, r, :] = f
            more = jnp.dot(f, zy, preferred_element_type=F32)
            total = more if total is None else total + more
        part[2 * g] = total[0:CAP].astype(BF)
        part[2 * g + 1] = total[CAP : 2 * CAP].astype(BF)

        @pl.when(g == 0)
        def _():
            t1.start()

        @pl.when(g == 1)
        def _():
            own_cap[...] = total[CAP : 2 * CAP]
            t3.start()
            for arrived, copy in zip(iway[0:2], icores[1:3]):
                arrived.wait_recv()
                copy.start()

        return carry

    lax.fori_loop(0, 2, two_slots, 0)

    def grad_rows(yl_, c_):
        f = coef[yl_, :, pl.ds(mo(c_ * PAD, PAD), PAD)]
        return lax.dot_general(f, caps[...], TN, preferred_element_type=F32)

    given = []
    for i, yl_ in enumerate((yl, 1 - yl)):
        img_send[i] = grad_rows(yl_, 1 - c)[0:IMG].astype(BF)
        given.append(go(img_send.at[i], img_recv.at[i], core))
        if i == 0:
            img_own[0] = grad_rows(yl_, c)[0:IMG]
    iway[2].wait_recv()
    icores[3].start()
    for copy in icores:
        copy.wait_recv()

    def gp_part(y_):
        return gp.at[y_ % 2, :, pl.ds(mo((y_ // 2) * 512, 512), 512)]

    def image_back(i, yl_):
        given[i].wait_recv()
        g = img_own[i] + img_recv[i].astype(F32)
        u = plane[pl.ds(mo((yl_ * 2 + c) * PAD, PAD), IMG), :].astype(F32)
        size = jnp.sum(u * u, axis=1, keepdims=True) + EPS
        along = jnp.sum(u * g, axis=1, keepdims=True)
        back = (g - u * (along / size)).astype(BF)
        grad = lax.dot_general(back, wimg[...], NT, preferred_element_type=F32)
        gp[yl_] = grad[0:HALF].astype(BF)
        for z_ in range(4):
            for yh_ in range(2):
                j = yh_ * 4 + z_
                gq[z_, i, yh_ * HALF : (yh_ + 1) * HALF, :] = grad[
                    HALF:IMG, j * SL : (j + 1) * SL
                ].astype(BF)

    def add(*refs):
        total = refs[0].astype(F32)
        for ref in refs[1:]:
            total = total + ref.astype(F32)
        return total

    image_back(0, yl)
    py1 = go(gp_part(ring(y, 2)), rpy.at[0], yf)
    qz = []

    def q_first(i):
        for n_, (step, target) in enumerate(((2, z2), (d, zf), (-d, zb))):
            qz.append(go(gq.at[ring(z, step), i], rqz.at[n_, i], target))

    q_first(0)
    img_own[1] = grad_rows(1 - yl, c)[0:IMG]
    image_back(1, 1 - yl)
    py3 = go(gp_part(ring(y, -d)), rpy.at[2], yb)
    q_first(1)
    t1.wait_recv()
    cap_mid[...] = (part[2].astype(F32) + cap_in[0].astype(F32)).astype(BF)
    t2 = go(cap_mid, cap_in.at[1], xf)
    py1.wait_recv()
    tpy[...] = add(gp_part(ring(y, d))[...], rpy[0]).astype(BF)
    py2 = go(tpy, rpy.at[1], yf)

    t2.wait_recv()
    t3.wait_recv()
    g = own_cap[...] + cap_in[1].astype(F32) + cap_in[2].astype(F32)
    raw = raw_cap[...]
    cap_scale = lax.rsqrt(jnp.sum(raw * raw, axis=1, keepdims=True) + EPS)
    u = raw * cap_scale
    along = jnp.sum(u * g, axis=1, keepdims=True)
    back = (cap_scale * (g - u * along)).astype(BF)
    res_cap[...] = lax.dot_general(
        back, wcap[...], NT, preferred_element_type=F32
    ).astype(BF)
    store_cap = load(4, res_cap, out_cap)

    py3.wait_recv()
    py2.wait_recv()
    own = add(gp_part(y)[...], rpy[1], rpy[2])
    for z_ in range(4):
        cut = own[:, z_ * SL : (z_ + 1) * SL]
        own_p2[z_] = cut
        gp2[z_] = cut.astype(BF)
    pz = [
        go(gp2.at[ring(z, 2)], rpz.at[0], z2),
        go(gp2.at[ring(z, d)], rpz.at[1], zf),
        go(gp2.at[ring(z, -d)], rpz.at[2], zb),
    ]
    for i in range(2):
        for copy in qz[3 * i : 3 * i + 3]:
            copy.wait_recv()
        own = add(gq[z, i], rqz[0, i], rqz[1, i], rqz[2, i])
        for yh_ in range(2):
            cut = own[yh_ * HALF : (yh_ + 1) * HALF]
            own_q2[i, yh_] = cut
            gq2[i, yh_] = cut.astype(BF)

    def q2(ref, y_):
        return ref.at[(y_ + y) % 2, y_ // 2]

    qy = [
        go(q2(gq2, ring(y, 2)), rqy.at[0], y2),
        go(q2(gq2, ring(y, d)), rqy.at[1], yf),
        go(q2(gq2, ring(y, -d)), rqy.at[2], yb),
    ]
    for copy in pz:
        copy.wait_recv()
    res_img[0:HALF, :] = (own_p2[z] + add(rpz[0], rpz[1], rpz[2])).astype(BF)
    for copy in qy:
        copy.wait_recv()
    res_img[HALF:IMG, :] = (own_q2[0, yh] + add(rqy[0], rqy[1], rqy[2])).astype(BF)
    store_img = load(5, res_img, out_img)
    for copy in copies:
        copy.wait_send()
    store_cap.wait()
    store_img.wait()


def finish(img, cap, out_img, out_cap):
    out_img[...] = img[...]
    out_cap[...] = cap[...]


COPIES = 96


def body(pic, sent, wp, ws, counts, sharp, bias):
    vm = pl.BlockSpec(memory_space=pltpu.VMEM)
    sm = pl.BlockSpec(memory_space=pltpu.SMEM)
    hbm = pl.BlockSpec(memory_space=pl.ANY)
    scratch = [
        ((IMG, D), BF),
        ((D, SL), BF),
        ((4 * CAP, D), BF),
        ((D, D), BF),
        ((D, D), BF),
        ((4 * PAD, D), BF),
        ((4 * CAP, D), BF),
        ((2, 4 * CAP, 2 * PAD), BF),
        ((2, 8, 2 * PAD), F32),
        ((2, 48, 128), F32),
        ((4, CAP, D), BF),
        ((CAP, D), F32),
        ((CAP, D), F32),
        ((3, CAP, D), BF),
        ((CAP, D), BF),
        ((2, IMG, D), BF),
        ((2, IMG, D), F32),
        ((2, IMG, D), BF),
        ((2, HALF, D), BF),
        ((4, 2, 2 * HALF, SL), BF),
        ((3, HALF, 512), BF),
        ((HALF, 512), BF),
        ((4, HALF, SL), BF),
        ((4, HALF, SL), F32),
        ((3, HALF, SL), BF),
        ((3, 2, 2 * HALF, SL), BF),
        ((2, 2, HALF, SL), BF),
        ((2, 2, HALF, SL), F32),
        ((3, HALF, SL), BF),
        ((IMG, SL), BF),
        ((CAP, D), BF),
    ]
    outs = (
        jax.ShapeDtypeStruct((IMG, SL), BF),
        jax.ShapeDtypeStruct((CAP, D), BF),
    )
    img, cap = pl.pallas_call(
        kernel,
        out_shape=outs,
        in_specs=[hbm] * 4 + [vm] + [sm] * 2,
        out_specs=(hbm, hbm),
        scratch_shapes=[pltpu.VMEM(shape, kind) for shape, kind in scratch]
        + [
            pltpu.SemaphoreType.DMA((COPIES,)),
            pltpu.SemaphoreType.DMA((COPIES,)),
            pltpu.SemaphoreType.DMA((6,)),
        ],
        compiler_params=pltpu.CompilerParams(
            collective_id=0, has_side_effects=True, vmem_limit_bytes=58 * 1024 * 1024
        ),
    )(pic, sent, wp, ws, counts.reshape(44, 128), sharp, bias)
    return pl.pallas_call(
        finish, out_shape=outs, in_specs=[vm, vm], out_specs=(vm, vm)
    )(img, cap)


def solution(mesh):
    in_specs = (
        P("dp", None),
        P(("dp", "tensor"), None),
        P(None, "tensor"),
        P(None, "tensor"),
        P(),
        P(),
        P(),
    )
    out_specs = (P("dp", "tensor"), P(("dp", "tensor"), None))
    return jax.shard_map(body, mesh=mesh, in_specs=in_specs, out_specs=out_specs, check_vma=False)
```

```python
import jax
import jax.numpy as jnp
from jax import lax
from jax.experimental import pallas as pl
from jax.experimental.pallas import tpu as pltpu
from jax.sharding import PartitionSpec as P

EPS = 1e-06
LOG2E = 1.4426950408889634
MESH = pl.DeviceIdType.MESH
BF = jnp.bfloat16
F32 = jnp.float32

D = 1024
IMG = 352
PAD = 384
HALF = 176
CUT = 256
CAP = 176
SL = 128
NT = (((1,), (1,)), ((), ()))
TN = (((0,), (0,)), ((), ()))


def mo(v, k):
    return pl.multiple_of(v, k)


def kernel(
    pic,
    sent,
    wp,
    ws,
    counts,
    sharp,
    bias,
    out_img,
    out_cap,
    pic_v,
    wp_v,
    feat,
    wcap,
    wimg,
    plane,
    caps,
    coef,
    vecs,
    starts,
    part,
    own_cap,
    raw_cap,
    cap_in,
    cap_mid,
    img_send,
    img_own,
    img_recv,
    gp,
    gq,
    rpy,
    tpy,
    gp2,
    own_p2,
    rpz,
    rqz,
    gq2,
    own_q2,
    rqy,
    res_img,
    res_cap,
    send_sem,
    recv_sem,
    load_sem,
):
    dp = lax.axis_index("dp")
    tensor = lax.axis_index("tensor")
    c = dp % 2
    x = (dp // 2) % 4
    yl = dp // 8
    yh = tensor // 4
    z = tensor % 4
    y = yh * 2 + yl
    d = 1 - 2 * c

    def dev(x_, y_, z_, c_):
        return ((y_ % 2) * 8 + x_ * 2 + c_, (y_ // 2) * 4 + z_)

    def ring(v, s):
        return (v + 4 + s) % 4

    def col(yh_, z_):
        return pl.ds(mo((yh_ * 4 + z_) * SL, SL), SL)

    x2 = dev(ring(x, 2), y, z, c)
    xf, xb = dev(ring(x, d), y, z, c), dev(ring(x, -d), y, z, c)
    yf, yb = dev(x, ring(y, d), z, c), dev(x, ring(y, -d), z, c)
    y2 = dev(x, ring(y, 2), z, c)
    zf, zb = dev(x, y, ring(z, d), c), dev(x, y, ring(z, -d), c)
    z2 = dev(x, y, ring(z, 2), c)
    core = dev(x, y, z, 1 - c)
    ym = dev(x, 3 - y, z, c)

    barrier = pltpu.get_barrier_semaphore()
    for other in (xf, xb, x2, yf, yb, y2, zf, zb, z2, core):
        pl.semaphore_signal(barrier, inc=1, device_id=other, device_id_type=MESH)

    def load(i, src, dst):
        copy = pltpu.make_async_copy(src, dst, load_sem.at[i])
        copy.start()
        return copy

    load_pic = load(0, pic, pic_v)
    load_wp = load(1, wp, wp_v)
    load_ws = load(2, ws, wcap.at[:, col(yh, z)])
    load_sent = load(3, sent, feat.at[3 * CAP : 4 * CAP])

    copies = []

    def make(src, dst, target):
        i = len(copies)
        copy = pltpu.make_async_remote_copy(
            src_ref=src,
            dst_ref=dst,
            send_sem=send_sem.at[i],
            recv_sem=recv_sem.at[i],
            device_id=target,
            device_id_type=MESH,
        )
        copies.append(copy)
        return copy

    def go(src, dst, target):
        copy = make(src, dst, target)
        copy.start()
        return copy

    def head_rows(x_):
        return pl.ds(mo((x_ * 2 + c) * 128, 128), 128)

    k_own = yl * 2 + c
    zero = jnp.zeros((PAD - IMG, D), BF)
    for k in range(4):
        plane[k * PAD + IMG : (k + 1) * PAD, :] = zero
    load_wp.wait()
    load_pic.wait()
    plane[pl.ds(mo(k_own * PAD, PAD), IMG), col(yh, z)] = jnp.dot(
        pic_v[...], wp_v[...], preferred_element_type=F32
    ).astype(BF)
    wimg[head_rows(x), col(yh, z)] = wp_v[head_rows(x), :]
    pl.semaphore_wait(barrier, 10)

    def p_rows(y_, lo=0, num=CUT):
        return pl.ds(mo(((y_ % 2) * 2 + c) * PAD + lo, 16), num)

    def q_rows(y_):
        return pl.ds(mo(((y_ % 2) * 2 + c) * PAD + CUT, 16), IMG - CUT)

    def p_z(z_, target):
        ref = plane.at[p_rows(y), col(yh, z_)]
        return go(ref, ref, target)

    def p_y(y_, target, lo=0, num=CUT):
        ref = plane.at[p_rows(y_, lo, num), pl.ds(mo((y_ // 2) * 512, 512), 512)]
        return go(ref, ref, target)

    def q_y(y_, target):
        ref = plane.at[q_rows(y_), col(y_ // 2, z)]
        return go(ref, ref, target)

    def q_z(z_, target):
        made = []
        for y_ in range(4):
            ref = plane.at[q_rows(y_), col(y_ // 2, z_)]
            made.append(go(ref, ref, target))
        return made

    hc = mo(c * 512, 512)

    half = ws.at[pl.ds(hc, 512)]
    here = wcap.at[pl.ds(hc, 512), col(yh, z)]

    def same(yh_, z_, target):
        ref = wcap.at[pl.ds(hc, 512), col(yh_, z_)]
        return go(ref, ref, target)

    def few(yh_, target):
        ref = wimg.at[head_rows(x), col(yh_, z)]
        return go(ref, ref, target)

    def many(x_, target, start=True):
        ref = wimg.at[head_rows(x_)]
        return (go if start else make)(ref, ref, target)

    def slot_rows(slot, lo, hi):
        return feat.at[slot * CAP + lo : slot * CAP + hi]

    ihead = [few(yh, target) for target in (ym, zf, zb, z2)]
    pz = [p_z(z, target) for target in (zf, zb, z2)]
    qy = [q_y(y, target) for target in (yf, yb, y2)]
    head = {"m": go(half, here, ym), "f": go(half, here, zf), "b": go(half, here, zb)}
    xf1 = go(sent.at[0:96], slot_rows(1, 0, 96), xf)
    xb1 = go(sent, slot_rows(2, 0, CAP), xb)
    xf2 = go(sent.at[96:CAP], slot_rows(1, 96, CAP), xf)

    for copy in qy:
        copy.wait_recv()
    qzf, qzb = q_z(z, zf), q_z(z, zb)
    ihead[0].wait_recv()
    ihead += [few(1 - yh, target) for target in (zf, zb, z2)]
    for copy in pz:
        copy.wait_recv()
    pyf0 = p_y(y, yf, 0, CUT // 2)
    pyb = p_y(y, yb)
    pyf1 = p_y(y, yf, CUT // 2, CUT // 2)
    swaps = [p_y(y, core)]
    head["m"].wait_recv()
    head_mf = same(1 - yh, z, zf)
    head_mb = same(1 - yh, z, zb)
    cores = [same(1 - yh, z, core)]
    head["f"].wait_recv()
    head_ff = same(yh, ring(z, -d), zf)
    cores.append(same(yh, ring(z, -d), core))
    xf1.wait_recv()
    xff1 = go(slot_rows(1, 0, 96), slot_rows(0, 0, 96), xf)
    pyf0.wait_recv()
    pyff0 = p_y(ring(y, -d), yf, 0, CUT // 2)
    head["b"].wait_recv()
    cores.append(same(yh, ring(z, d), core))
    for copy in qzf:
        copy.wait_recv()
    qzff = q_z(ring(z, -d), zf)
    head_mf.wait_recv()
    head_mff = same(1 - yh, ring(z, -d), zf)
    cores.append(same(1 - yh, ring(z, -d), core))
    xf2.wait_recv()
    xff2 = go(slot_rows(1, 96, CAP), slot_rows(0, 96, CAP), xf)
    for copy in ihead[1:]:
        copy.wait_recv()
    icores = [many(x, core)]
    icores += [many(ring(x, step), core, False) for step in (-d, d, 2)]
    iway = [many(x, target) for target in (xf, xb, x2)]
    pyf1.wait_recv()
    pyff1 = p_y(ring(y, -d), yf, CUT // 2, CUT // 2)
    swaps.append(p_y(ring(y, -d), core))

    n = counts[...].astype(F32)
    nb = n.astype(BF)
    a = lax.broadcasted_iota(jnp.int32, (128, 128), 0)
    b = lax.broadcasted_iota(jnp.int32, (128, 128), 1)
    upto = jnp.dot(nb, (a < b).astype(F32).astype(BF), preferred_element_type=F32)
    a = lax.broadcasted_iota(jnp.int32, (44, 44), 0)
    b = lax.broadcasted_iota(jnp.int32, (44, 44), 1)
    before = jnp.dot((b < a).astype(F32).astype(BF), nb, preferred_element_type=F32)
    starts[0, 0:44, :] = upto + jnp.sum(before, axis=1, keepdims=True)
    starts[1, 0:44, :] = n
    starts[0, 44:48, :] = jnp.full((4, 128), -1.0, F32)
    starts[1, 44:48, :] = jnp.full((4, 128), 1.0, F32)

    t = sharp[0]
    shift = bias[0] * LOG2E
    ones = jnp.ones((8, D), BF)
    even = x % 2 == 0

    def block_vec(which, yl_, c_):
        row = (yl_ * 4 + x) * 2 + c_
        q = (row * 11) // 4
        v = jnp.concatenate([starts[which, pl.ds(q + i, 1), :] for i in range(4)], axis=1)
        cuts = [((2 * p + 3 * c_) % 4) * 32 for p in range(2)]
        return jnp.where(even, v[:, cuts[0] : cuts[0] + PAD], v[:, cuts[1] : cuts[1] + PAD])

    for yl_ in range(2):
        for c_ in range(2):
            first = block_vec(0, yl_, c_)
            num = block_vec(1, yl_, c_)
            lanes = slice(c_ * PAD, (c_ + 1) * PAD)
            vecs[yl_, 3:4, lanes] = first
            vecs[yl_, 4:5, lanes] = first + num
            vecs[yl_, 5:6, lanes] = -1.0 / num

    def scales(yl_, c_):
        zk = plane[pl.ds(mo((yl_ * 2 + c_) * PAD, PAD), PAD), :]
        square = lax.dot_general(ones, zk * zk, NT, preferred_element_type=F32)
        scale = t * lax.rsqrt(square[0:1, :] + EPS)
        lanes = pl.ds(mo(c_ * PAD, PAD), PAD)
        vecs[yl_, 0:1, lanes] = scale * LOG2E
        vecs[yl_, 1:2, lanes] = scale
        vecs[yl_, 2:3, lanes] = scale * vecs[yl_, 5:6, lanes]

    head_ff.wait_recv()
    cores.append(same(yh, ring(z, 2), core))
    head_mb.wait_recv()
    cores.append(same(1 - yh, ring(z, d), core))
    pyb.wait_recv()
    swaps.append(p_y(ring(y, d), core))
    head_mff.wait_recv()
    cores.append(same(1 - yh, ring(z, 2), core))
    for copy in cores:
        copy.wait_recv()

    load_ws.wait()
    load_sent.wait()

    def embed(rows):
        raw = jnp.dot(feat[rows, :], wcap[...], preferred_element_type=F32)
        cap_scale = lax.rsqrt(jnp.sum(raw * raw, axis=1, keepdims=True) + EPS)
        caps[rows, :] = (raw * cap_scale).astype(BF)
        return raw

    xb1.wait_recv()
    raw_cap[...] = embed(slice(2 * CAP, 4 * CAP))[CAP : 2 * CAP]
    pyff0.wait_recv()
    pyff1.wait_recv()
    swaps.append(p_y(ring(y, 2), core))
    for copy in qzb + qzff:
        copy.wait_recv()
    for yl_ in range(2):
        ref = plane.at[q_rows(yl_)]
        swaps.append(go(ref, ref, core))
    for yl_ in range(2):
        scales(yl_, c)
    xff1.wait_recv()
    xff2.wait_recv()
    embed(slice(0, 2 * CAP))
    for copy in swaps:
        copy.wait_recv()
    for yl_ in range(2):
        scales(yl_, 1 - c)

    t1 = make(part.at[0], cap_in.at[0], xf)
    t3 = make(part.at[1], cap_in.at[2], xb)

    def base(step):
        return (((yl * 4 + ring(x, step)) * 2 + c) * 8 + tensor) * CAP

    def two_slots(g, carry):
        low = jnp.where(g == 0, base(2), base(d))
        high = jnp.where(g == 0, base(-d), base(0))
        i = lax.broadcasted_iota(jnp.int32, (2 * CAP, 1), 0)
        number = (i + jnp.where(i < CAP, low, high - CAP)).astype(F32)
        r = pl.ds(mo(g * 2 * CAP, 2 * CAP), 2 * CAP)
        total = None
        for yl_ in range(2):
            zy = plane[yl_ * 2 * PAD : (yl_ + 1) * 2 * PAD, :]
            s = lax.dot_general(caps[r, :], zy, NT, preferred_element_type=F32)
            l2 = s * vecs[yl_, 0:1, :] + shift
            inside = (number >= vecs[yl_, 3:4, :]) & (number < vecs[yl_, 4:5, :])
            e = jnp.exp2(jnp.where(inside, l2, -l2))
            w = jnp.where(inside, vecs[yl_, 2:3, :], vecs[yl_, 1:2, :])
            f = (w / (1.0 + e)).astype(BF)
            coef[yl_, r, :] = f
            more = jnp.dot(f, zy, preferred_element_type=F32)
            total = more if total is None else total + more
        part[2 * g] = total[0:CAP].astype(BF)
        part[2 * g + 1] = total[CAP : 2 * CAP].astype(BF)

        @pl.when(g == 0)
        def _():
            t1.start()

        @pl.when(g == 1)
        def _():
            own_cap[...] = total[CAP : 2 * CAP]
            t3.start()
            for arrived, copy in zip(iway[0:2], icores[1:3]):
                arrived.wait_recv()
                copy.start()

        return carry

    lax.fori_loop(0, 2, two_slots, 0)

    def grad_rows(yl_, c_):
        f = coef[yl_, :, pl.ds(mo(c_ * PAD, PAD), PAD)]
        return lax.dot_general(f, caps[...], TN, preferred_element_type=F32)

    given = []
    for i, yl_ in enumerate((yl, 1 - yl)):
        img_send[i] = grad_rows(yl_, 1 - c)[0:IMG].astype(BF)
        given.append(go(img_send.at[i], img_recv.at[i], core))
        if i == 0:
            img_own[0] = grad_rows(yl_, c)[0:IMG]
    iway[2].wait_recv()
    icores[3].start()
    for copy in icores:
        copy.wait_recv()

    def gp_part(y_):
        return gp.at[y_ % 2, :, pl.ds(mo((y_ // 2) * 512, 512), 512)]

    def image_back(i, yl_):
        given[i].wait_recv()
        g = img_own[i] + img_recv[i].astype(F32)
        u = plane[pl.ds(mo((yl_ * 2 + c) * PAD, PAD), IMG), :].astype(F32)
        size = jnp.sum(u * u, axis=1, keepdims=True) + EPS
        along = jnp.sum(u * g, axis=1, keepdims=True)
        back = (g - u * (along / size)).astype(BF)
        grad = lax.dot_general(back, wimg[...], NT, preferred_element_type=F32)
        gp[yl_] = grad[0:HALF].astype(BF)
        for z_ in range(4):
            for yh_ in range(2):
                j = yh_ * 4 + z_
                gq[z_, i, yh_ * HALF : (yh_ + 1) * HALF, :] = grad[
                    HALF:IMG, j * SL : (j + 1) * SL
                ].astype(BF)

    def add(*refs):
        total = refs[0].astype(F32)
        for ref in refs[1:]:
            total = total + ref.astype(F32)
        return total

    image_back(0, yl)
    py1 = go(gp_part(ring(y, 2)), rpy.at[0], yf)
    qz = []

    def q_first(i):
        for n_, (step, target) in enumerate(((2, z2), (d, zf), (-d, zb))):
            qz.append(go(gq.at[ring(z, step), i], rqz.at[n_, i], target))

    q_first(0)
    img_own[1] = grad_rows(1 - yl, c)[0:IMG]
    image_back(1, 1 - yl)
    py3 = go(gp_part(ring(y, -d)), rpy.at[2], yb)
    q_first(1)
    t1.wait_recv()
    cap_mid[...] = (part[2].astype(F32) + cap_in[0].astype(F32)).astype(BF)
    t2 = go(cap_mid, cap_in.at[1], xf)
    py1.wait_recv()
    tpy[...] = add(gp_part(ring(y, d))[...], rpy[0]).astype(BF)
    py2 = go(tpy, rpy.at[1], yf)

    t2.wait_recv()
    t3.wait_recv()
    g = own_cap[...] + cap_in[1].astype(F32) + cap_in[2].astype(F32)
    raw = raw_cap[...]
    cap_scale = lax.rsqrt(jnp.sum(raw * raw, axis=1, keepdims=True) + EPS)
    u = raw * cap_scale
    along = jnp.sum(u * g, axis=1, keepdims=True)
    back = (cap_scale * (g - u * along)).astype(BF)
    res_cap[...] = lax.dot_general(
        back, wcap[...], NT, preferred_element_type=F32
    ).astype(BF)
    store_cap = load(4, res_cap, out_cap)

    py3.wait_recv()
    py2.wait_recv()
    own = add(gp_part(y)[...], rpy[1], rpy[2])
    for z_ in range(4):
        cut = own[:, z_ * SL : (z_ + 1) * SL]
        own_p2[z_] = cut
        gp2[z_] = cut.astype(BF)
    pz = [
        go(gp2.at[ring(z, 2)], rpz.at[0], z2),
        go(gp2.at[ring(z, d)], rpz.at[1], zf),
        go(gp2.at[ring(z, -d)], rpz.at[2], zb),
    ]
    for i in range(2):
        for copy in qz[3 * i : 3 * i + 3]:
            copy.wait_recv()
        own = add(gq[z, i], rqz[0, i], rqz[1, i], rqz[2, i])
        for yh_ in range(2):
            cut = own[yh_ * HALF : (yh_ + 1) * HALF]
            own_q2[i, yh_] = cut
            gq2[i, yh_] = cut.astype(BF)

    def q2(ref, y_):
        return ref.at[(y_ + y) % 2, y_ // 2]

    qy = [
        go(q2(gq2, ring(y, 2)), rqy.at[0], y2),
        go(q2(gq2, ring(y, d)), rqy.at[1], yf),
        go(q2(gq2, ring(y, -d)), rqy.at[2], yb),
    ]
    for copy in pz:
        copy.wait_recv()
    res_img[0:HALF, :] = (own_p2[z] + add(rpz[0], rpz[1], rpz[2])).astype(BF)
    for copy in qy:
        copy.wait_recv()
    res_img[HALF:IMG, :] = (own_q2[0, yh] + add(rqy[0], rqy[1], rqy[2])).astype(BF)
    store_img = load(5, res_img, out_img)
    for copy in copies:
        copy.wait_send()
    store_cap.wait()
    store_img.wait()


def finish(img, cap, out_img, out_cap):
    out_img[...] = img[...]
    out_cap[...] = cap[...]


COPIES = 96


def body(pic, sent, wp, ws, counts, sharp, bias):
    vm = pl.BlockSpec(memory_space=pltpu.VMEM)
    sm = pl.BlockSpec(memory_space=pltpu.SMEM)
    hbm = pl.BlockSpec(memory_space=pl.ANY)
    scratch = [
        ((IMG, D), BF),
        ((D, SL), BF),
        ((4 * CAP, D), BF),
        ((D, D), BF),
        ((D, D), BF),
        ((4 * PAD, D), BF),
        ((4 * CAP, D), BF),
        ((2, 4 * CAP, 2 * PAD), BF),
        ((2, 8, 2 * PAD), F32),
        ((2, 48, 128), F32),
        ((4, CAP, D), BF),
        ((CAP, D), F32),
        ((CAP, D), F32),
        ((3, CAP, D), BF),
        ((CAP, D), BF),
        ((2, IMG, D), BF),
        ((2, IMG, D), F32),
        ((2, IMG, D), BF),
        ((2, HALF, D), BF),
        ((4, 2, 2 * HALF, SL), BF),
        ((3, HALF, 512), BF),
        ((HALF, 512), BF),
        ((4, HALF, SL), BF),
        ((4, HALF, SL), F32),
        ((3, HALF, SL), BF),
        ((3, 2, 2 * HALF, SL), BF),
        ((2, 2, HALF, SL), BF),
        ((2, 2, HALF, SL), F32),
        ((3, HALF, SL), BF),
        ((IMG, SL), BF),
        ((CAP, D), BF),
    ]
    outs = (
        jax.ShapeDtypeStruct((IMG, SL), BF),
        jax.ShapeDtypeStruct((CAP, D), BF),
    )
    img, cap = pl.pallas_call(
        kernel,
        out_shape=outs,
        in_specs=[hbm] * 4 + [vm] + [sm] * 2,
        out_specs=(hbm, hbm),
        scratch_shapes=[pltpu.VMEM(shape, kind) for shape, kind in scratch]
        + [
            pltpu.SemaphoreType.DMA((COPIES,)),
            pltpu.SemaphoreType.DMA((COPIES,)),
            pltpu.SemaphoreType.DMA((6,)),
        ],
        compiler_params=pltpu.CompilerParams(
            collective_id=0, has_side_effects=True, vmem_limit_bytes=58 * 1024 * 1024
        ),
    )(pic, sent, wp, ws, counts.reshape(44, 128), sharp, bias)
    return pl.pallas_call(
        finish, out_shape=outs, in_specs=[vm, vm], out_specs=(vm, vm)
    )(img, cap)


def solution(mesh):
    in_specs = (
        P("dp", None),
        P(("dp", "tensor"), None),
        P(None, "tensor"),
        P(None, "tensor"),
        P(),
        P(),
        P(),
    )
    out_specs = (P("dp", "tensor"), P(("dp", "tensor"), None))
    return jax.shard_map(body, mesh=mesh, in_specs=in_specs, out_specs=out_specs, check_vma=False)
```
